32 devices in a mesh: seq: 8 (over z, x), tile: 4 (over y, core).
Axes of the slice: x: 2, y: 2, z: 4, core: 2. Of those that a mesh axis runs over, the one named last changes fastest.
Arguments:
- query_feat: float32 [1536, 4096], P('seq', 'tile'), may hold values from -6 to 6
- key_feat: float32 [1536, 4096], P('seq', 'tile'), may hold values from -6 to 6
- value_feat: float32 [1536, 4096], P('seq', 'tile'), may hold values from -6 to 6
- short_filter: float32 [3, 7, 4096], P(None, None, 'tile'), may hold values from -3 to 3
- medium_filter: float32 [128, 4096], P(None, 'tile'), may hold values from -0.6 to 0.6
- out_weight: bfloat16 [4096, 4096], P('tile'), may hold values from -0.09375 to 0.09375
- cotangent: bfloat16 [1536, 4096], P('seq', 'tile'), may hold values from -6 to 6
Outputs:
- block_out: float32 [1536, 4096], P('seq', 'tile')
- grad_query: float32 [1536, 4096], P('seq', 'tile')
- grad_key: float32 [1536, 4096], P('seq', 'tile')
- grad_value: float32 [1536, 4096], P('seq', 'tile')
- grad_short: float32 [3, 7, 4096], P(None, None, 'tile')
- grad_medium: float32 [128, 4096], P(None, 'tile')
The draws below stay inside these ranges and needn't reach their ends.
All inputs are finite; a program needn't handle non-finite values.
Results may differ from the reference program's by a relative error of at most 0.0029.
Values may be sent and summed in bfloat16 or wider, within the bound.
A program may use at most 64 MiB of HBM per device.

```python
import math
import jax
import jax.numpy as jnp
from jax import lax

D = 4096
C = 4096
SHORT = 7
MEDIUM = 128
TOKENS = 1536


def level_of(key, shape, split, smallest, largest):
    factor_of, own = 1.0, jax.random.fold_in(key, 6)
    for dim, shards_of in split:
        steps = jnp.exp(jax.random.uniform(jax.random.fold_in(own, dim), (shards_of,), jnp.float32, smallest / len(split), largest / len(split)))
        factor_of = factor_of * jnp.repeat(steps, shape[dim] // shards_of).reshape([-1 if axis == dim else 1 for axis in range(len(shape))])
    return factor_of


def gaussian(key, extent, width, limit, shards=(), kind=jnp.bfloat16):
    array = width * jax.random.normal(key, extent, jnp.float32)
    if shards:
        array = array * level_of(key, extent, shards, -0.22, 0.18)
    return jnp.clip(array, -limit, limit).astype(kind)


def setup_inputs(seed: int = 0) -> dict:
    splits = jax.random.split(jax.random.key(seed), 8)
    return {
        "query_feat": gaussian(splits[0], (TOKENS, C), 1.0, 6.0, ((0, 8), (1, 4)), jnp.float32),
        "key_feat": gaussian(splits[1], (TOKENS, C), 1.0, 6.0, ((0, 8), (1, 4)), jnp.float32),
        "value_feat": gaussian(splits[2], (TOKENS, C), 1.0, 6.0, ((0, 8), (1, 4)), jnp.float32),
        "short_filter": gaussian(splits[3], (3, SHORT, C), 0.4, 3.0, ((2, 4),), jnp.float32),
        "medium_filter": gaussian(splits[4], (MEDIUM, C), 0.1, 0.6, ((1, 4),), jnp.float32),
        "out_weight": gaussian(splits[5], (C, D), C ** -0.5, 0.09375, ((0, 4),)),
        "cotangent": gaussian(splits[6], (TOKENS, D), 1.0, 6.0, ((0, 8), (1, 4))),
    }


def causal_conv(extended, filter_taps):
    taps = filter_taps.shape[0]
    count = extended.shape[0] - taps + 1

    def add_tap(index, total):
        start = (taps - 1 - index).astype(jnp.int32)
        return total + filter_taps[index] * lax.dynamic_slice_in_dim(extended, start, count, 0)
    return lax.fori_loop(jnp.int32(0), jnp.int32(taps), add_tap, jnp.zeros((count, extended.shape[1]), extended.dtype))

def reverse_conv(extended, filter_taps):
    taps = filter_taps.shape[0]
    count = extended.shape[0] - taps + 1

    def add_tap(index, total):
        start = index.astype(jnp.int32)
        return total + filter_taps[index] * lax.dynamic_slice_in_dim(extended, start, count, 0)
    return lax.fori_loop(jnp.int32(0), jnp.int32(taps), add_tap, jnp.zeros((count, extended.shape[1]), extended.dtype))

def taps_grad(extended, grad_rows):
    count = grad_rows.shape[0]
    taps = extended.shape[0] - count + 1

    def one_tap(index):
        start = (taps - 1 - index).astype(jnp.int32)
        return lax.optimization_barrier(jnp.sum(grad_rows * lax.dynamic_slice_in_dim(extended, start, count, 0), axis=0))
    return lax.map(one_tap, jnp.arange(taps, dtype=jnp.int32))

def reference(query_feat, key_feat, value_feat, short_filter, medium_filter, out_weight, cotangent):
    short_len = short_filter.shape[1]
    medium_len = medium_filter.shape[0]
    front_short = ((short_len - 1, 0), (0, 0))
    back_short = ((0, short_len - 1), (0, 0))
    query_ext = jnp.pad(query_feat, front_short)
    key_ext = jnp.pad(key_feat, front_short)
    value_ext = jnp.pad(value_feat, front_short)
    query_short = causal_conv(query_ext, short_filter[0])
    key_short = causal_conv(key_ext, short_filter[1])
    value_short = causal_conv(value_ext, short_filter[2])
    gated = key_short * value_short
    gated_ext = jnp.pad(gated, ((medium_len - 1, 0), (0, 0)))
    mixed = causal_conv(gated_ext, medium_filter)
    gated_out = (query_short * mixed).astype(jnp.bfloat16)
    block_out = jnp.dot(gated_out, out_weight, preferred_element_type=jnp.float32)
    grad_gated = jnp.dot(cotangent, out_weight.T, preferred_element_type=jnp.float32)
    grad_qshort = grad_gated * mixed
    grad_mixed = grad_gated * query_short
    grad_prod = reverse_conv(jnp.pad(grad_mixed, ((0, medium_len - 1), (0, 0))), medium_filter)
    grad_kshort = grad_prod * value_short
    grad_vshort = grad_prod * key_short
    grad_query = reverse_conv(jnp.pad(grad_qshort, back_short), short_filter[0])
    grad_key = reverse_conv(jnp.pad(grad_kshort, back_short), short_filter[1])
    grad_value = reverse_conv(jnp.pad(grad_vshort, back_short), short_filter[2])
    norm_scale = 1.0 / math.sqrt(TOKENS)
    grad_medium = taps_grad(gated_ext, grad_mixed) * norm_scale
    grad_short = jnp.stack([taps_grad(query_ext, grad_qshort), taps_grad(key_ext, grad_kshort), taps_grad(value_ext, grad_vshort)]) * norm_scale
    return (block_out, grad_query, grad_key, grad_value, grad_short, grad_medium)
```

```python
import functools
import math

import jax
import jax.numpy as jnp
import ml_dtypes
import numpy as np
from jax import lax
from jax.experimental import pallas as pl
from jax.experimental.pallas import tpu as pltpu
from jax.sharding import PartitionSpec as P

MESH = pl.DeviceIdType.MESH
F32 = jnp.float32
BF16 = jnp.bfloat16
LANES = 128
WIDE = 256
EDGE = 8


def split_const(matrix):
    hi = matrix.astype(np.float32).astype(ml_dtypes.bfloat16)
    lo = (matrix - hi.astype(np.float64)).astype(np.float32).astype(ml_dtypes.bfloat16)
    return np.stack([hi, lo])


def dft_consts(rows, taps):
    size = rows + taps
    theta = 2.0 * np.pi * (np.arange(size // 2) + 0.5) / size

    def forward(first, last):
        angle = theta[:, None] * np.arange(first, last)[None, :]
        return split_const(np.concatenate([np.cos(angle), -np.sin(angle)], axis=0))

    def inverse(first, last):
        angle = np.arange(first, last)[:, None] * theta[None, :]
        return split_const(np.concatenate([np.cos(angle), -np.sin(angle)], axis=1) * (2.0 / size))

    return (
        forward(0, taps),
        forward(taps, size),
        forward(0, rows),
        forward(rows, size),
        inverse(taps, size),
        inverse(0, rows),
        inverse(-taps, 0),
    )


def mm(a, b):
    return jnp.dot(a, b, preferred_element_type=F32)


def dft_wide(matrix, x):
    hi = x.astype(BF16)
    lo = (x - hi.astype(F32)).astype(BF16)
    return mm(matrix[0], hi) + mm(matrix[1], hi) + mm(matrix[0], lo)


def dft_half(matrix, x):
    return mm(matrix[0], x) + mm(matrix[1], x)


def times(a, b):
    half = a.shape[0] // 2
    ar, ai, br, bi = a[:half], a[half:], b[:half], b[half:]
    return jnp.concatenate([ar * br - ai * bi, ar * bi + ai * br], axis=0)


def conj_times(a, b):
    half = a.shape[0] // 2
    ar, ai, br, bi = a[:half], a[half:], b[:half], b[half:]
    return jnp.concatenate([ar * br + ai * bi, ar * bi - ai * br], axis=0)


def low_bit(r):
    return (r & -r).bit_length() - 1


def kernel(
    n_seq, n_tile, n_own, scale,
    xq, xk, xv, cot, weight, sf, mf, fw_taps, fw_tail, fw_head, fw_after, inv_tail, inv_head, inv_taps,
    out_ref, gq_ref, gk_ref, gv_ref, gs_ref, gm_ref,
    xe, wv, cotv, hspec, gspec, vspec, ks, vs, qs, gated, gg, gmix, ge, gout, part,
    ghalo_s, ghalo_r, mhalo_s, mhalo_r, psend, precv, msend, mrecv, mall, ssend, srecv, sall,
    x_sem, w_sem, c_sem, xh_ss, xh_rs, ca_ss, ca_rs, gh_ss, gh_rs, mh_ss, mh_rs,
    eh_ss, eh_rs, p_ss, p_rs, m_ss, m_rs, ma_ss, ma_rs, s_ss, s_rs, sa_ss, sa_rs,
):
    rows, width = ks.shape
    taps = mf.shape[0]
    short = sf.shape[1]
    block = cotv.shape[2]
    bits = n_tile.bit_length() - 1
    x_refs = (xq, xk, xv)
    me = lax.axis_index("seq")
    tile = lax.axis_index("tile")

    def flip(k):
        return tile + (1 << k) - (2 << k) * ((tile // (1 << k)) % 2)

    def relative(r):
        index = tile * 0
        for k in range(bits):
            bit = (tile // (1 << k)) % 2
            index = index + (1 << k) * ((1 - bit) if (r >> k) & 1 else bit)
        return index

    def to_seq(src, dst, send, recv, index):
        return pltpu.make_async_remote_copy(src, dst, send, recv, device_id={"seq": index}, device_id_type=MESH)

    def to_tile(src, dst, send, recv, k):
        return pltpu.make_async_remote_copy(src, dst, send, recv, device_id={"tile": flip(k)}, device_id_type=MESH)

    def lanes(c, size):
        return pl.ds(pl.multiple_of(c * size, size), size)

    def over(size, body):
        def step(c, carry):
            body(c, lanes(c, size))
            return carry
        lax.fori_loop(0, width // size, step, 0)

    x_copies = [pltpu.make_async_copy(x_refs[i], xe.at[i, pl.ds(EDGE, rows)], x_sem.at[i]) for i in range(3)]
    for copy in x_copies:
        copy.start()
    own_cot = pltpu.make_async_copy(cot, cotv.at[0], c_sem)
    own_cot.start()
    w_copies = []
    for r in range(n_tile):
        columns = pl.ds(pl.multiple_of(relative(r) * block, block), block)
        w_copies.append(pltpu.make_async_copy(weight.at[:, columns], wv.at[r], w_sem.at[r]))
        w_copies[-1].start()

    barrier = pltpu.get_barrier_semaphore()

    def greet(d, carry):
        pl.semaphore_signal(barrier, inc=1, device_id={"seq": (me + d) % n_seq}, device_id_type=MESH)
        return carry
    lax.fori_loop(1, n_seq, greet, 0)
    for k in range(bits):
        pl.semaphore_signal(barrier, inc=1, device_id={"tile": flip(k)}, device_id_type=MESH)
    pl.semaphore_wait(barrier, n_seq - 1 + bits)

    has_next = me < n_seq - 1
    has_prev = me > 0
    nxt = (me + 1) % n_seq
    prv = (me + n_seq - 1) % n_seq

    x_halo = [
        to_seq(x_refs[i].at[pl.ds(rows - EDGE, EDGE)], xe.at[i, pl.ds(0, EDGE)], xh_ss.at[i], xh_rs.at[i], nxt)
        for i in range(3)
    ]

    @pl.when(has_next)
    def _():
        for i in (1, 2, 0):
            x_halo[i].start()

    gather = {}
    for k in reversed(range(bits)):
        gather[1 << k] = to_tile(cot, cotv.at[1 << k], ca_ss.at[1 << k], ca_rs.at[1 << k], k)
        gather[1 << k].start()

    @pl.when(jnp.logical_not(has_prev))
    def _():
        for i in range(3):
            xe[i, pl.ds(0, EDGE), :] = jnp.zeros((EDGE, width), F32)
        ghalo_r[...] = jnp.zeros_like(ghalo_r)

    @pl.when(jnp.logical_not(has_next))
    def _():
        for i in range(3):
            ge[i, pl.ds(rows, EDGE), :] = jnp.zeros((EDGE, width), F32)
        mhalo_r[...] = jnp.zeros_like(mhalo_r)

    def filter_spectrum(c, ls):
        hspec[:, ls] = dft_wide(fw_taps, mf[:, ls])
    over(WIDE, filter_spectrum)

    for copy in x_copies:
        copy.wait()

    @pl.when(has_prev)
    def _():
        for i in range(3):
            x_halo[i].wait_recv()

    def short_conv(i, ls):
        total = sf[i, pl.ds(0, 1), ls] * xe[i, pl.ds(EDGE, rows), ls]
        for j in range(1, short):
            total = total + sf[i, pl.ds(j, 1), ls] * xe[i, pl.ds(EDGE - j, rows), ls]
        return total

    def key_value(c, ls):
        k_rows = short_conv(1, ls)
        ks[:, ls] = k_rows
        v_rows = short_conv(2, ls)
        vs[:, ls] = v_rows
        product = k_rows * v_rows
        gated[:, ls] = product
        ghalo_s[:, ls] = product[rows - taps:].astype(BF16)
    over(LANES, key_value)

    ghalo = to_seq(ghalo_s, ghalo_r, gh_ss, gh_rs, nxt)

    @pl.when(has_next)
    def _():
        ghalo.start()

    def query(c, ls):
        qs[:, ls] = short_conv(0, ls)
    over(LANES, query)

    def gated_spectrum(c, ls):
        gspec[:, ls] = dft_wide(fw_tail, gated[:, ls])
    over(WIDE, gated_spectrum)

    for r in range(n_tile):
        if r == 0:
            own_cot.wait()
        else:
            gather[r].wait_recv()
            for k in reversed(range(low_bit(r))):
                slot = r + (1 << k)
                gather[slot] = to_tile(cotv.at[r], cotv.at[slot], ca_ss.at[slot], ca_rs.at[slot], k)
                gather[slot].start()
        w_copies[r].wait()

        def grad_block(c, ls, r=r):
            term = lax.dot_general(
                cotv[r], wv[r, ls, :], (((1,), (1,)), ((), ())), preferred_element_type=F32
            )
            if r > 0:
                term = term + gg[:, ls]
            gg[:, ls] = term
            if r == n_tile - 1:
                grad_mixed = term * qs[:, ls]
                gmix[:, ls] = grad_mixed
                mhalo_s[:, ls] = grad_mixed[:taps].astype(BF16)
        over(WIDE, grad_block)

    mhalo = to_seq(mhalo_s, mhalo_r, mh_ss, mh_rs, prv)

    @pl.when(has_prev)
    def _():
        mhalo.start()

    @pl.when(has_prev)
    def _():
        ghalo.wait_recv()

    def mixed_rows(c, ls):
        spectrum = gspec[:, ls] + dft_half(fw_taps, ghalo_r[:, ls])
        gspec[:, ls] = spectrum
        mixed = dft_wide(inv_tail, times(spectrum, hspec[:, ls]))
        gout[:, ls] = (qs[:, ls] * mixed).astype(BF16)
        ge[0, pl.ds(0, rows), ls] = gg[:, ls] * mixed
    over(WIDE, mixed_rows)

    e_halo = [
        to_seq(ge.at[i, pl.ds(0, EDGE)], ge.at[i, pl.ds(rows, EDGE)], eh_ss.at[i], eh_rs.at[i], prv) for i in range(3)
    ]

    @pl.when(has_prev)
    def _():
        e_halo[0].start()

    scatter = {}

    def project(r):
        def body(c, carry):
            ds = lanes(c, WIDE)
            term = mm(gout[...], wv[r, :, ds])
            if r & 1:
                psend[r, :, ds] = term.astype(BF16)
            else:
                part[r, :, ds] = term
            return carry
        lax.fori_loop(0, block // WIDE, body, 0)

    def send_sum(r):
        k = low_bit(r)
        scatter[r] = to_tile(psend.at[r], precv.at[r], p_ss.at[r], p_rs.at[r], k)
        scatter[r].start()

    for r in sorted(range(n_tile), key=lambda r: (1 - (r & 1), -r)):
        project(r)
        if r & 1:
            send_sum(r)

    per_wide = WIDE // LANES

    def medium_grad(c, ls):
        v_spec = dft_wide(fw_head, gmix[:, ls])
        vspec[:, ls] = v_spec
        terms = dft_wide(inv_taps, conj_times(gspec[:, ls], v_spec)) * scale
        for p in range(per_wide):
            msend[c * per_wide + p] = terms[:, p * LANES:(p + 1) * LANES]
    over(WIDE, medium_grad)

    def owner_copy(send, recv, ss, rs, d):
        return to_seq(send.at[(me + d) % n_seq], recv.at[d], ss.at[d], rs.at[d], (me + d) % n_seq)

    def if_owner(index, body):
        if n_own == n_seq:
            body()
        else:
            pl.when(index < n_own)(body)

    def peers(body):
        def step(d, carry):
            body(d)
            return carry
        lax.fori_loop(1, n_seq, step, 0)

    def to_owners(send, recv, ss, rs):
        peers(lambda d: if_owner((me + d) % n_seq, lambda: owner_copy(send, recv, ss, rs, d).start()))

    def from_owner_copy(full, ss, rs, d):
        return to_seq(full.at[me], full.at[me], ss.at[d], rs.at[d], (me + d) % n_seq)

    def owner_sum(send, recv, ss, rs, full, f_ss, f_rs):
        def body():
            full[me] = send[me].astype(F32)

            def add(d):
                owner_copy(send, recv, ss, rs, d).wait_recv()
                full[me] = full[me] + recv[d].astype(F32)
            peers(add)
            peers(lambda d: from_owner_copy(full, f_ss, f_rs, d).start())
        if_owner(me, body)

    def from_owners(full, ss, rs):
        def wait(d):
            source = (me + n_seq - d) % n_seq
            if_owner(source, lambda: to_seq(full.at[source], full.at[source], ss.at[d], rs.at[d], source).wait_recv())
        peers(wait)

    def end_sends(send, recv, ss, rs, full, f_ss, f_rs):
        peers(lambda d: if_owner((me + d) % n_seq, lambda: owner_copy(send, recv, ss, rs, d).wait_send()))
        if_owner(me, lambda: peers(lambda d: from_owner_copy(full, f_ss, f_rs, d).wait_send()))

    medium_set = (msend, mrecv, m_ss, m_rs, mall, ma_ss, ma_rs)
    short_set = (ssend, srecv, s_ss, s_rs, sall, sa_ss, sa_rs)
    to_owners(*medium_set[:4])

    def add_sums(r, first, last):
        total = part[r]
        for k in range(first, last):
            scatter[r + (1 << k)].wait_recv()
            total = total + precv[r + (1 << k)].astype(F32)
        return total

    def step_sums(k):
        for r in range(1 << k, n_tile, 2 << k):
            psend[r] = add_sums(r, 0, k).astype(BF16)
            send_sum(r)

    for k in range(1, bits):
        step_sums(k)

    @pl.when(has_next)
    def _():
        mhalo.wait_recv()

    def product_rows(c, ls):
        spectrum = vspec[:, ls] + dft_half(fw_after, mhalo_r[:, ls])
        grad_prod = dft_wide(inv_head, conj_times(hspec[:, ls], spectrum))
        ge[1, pl.ds(0, rows), ls] = grad_prod * vs[:, ls]
        ge[2, pl.ds(0, rows), ls] = grad_prod * ks[:, ls]
    over(WIDE, product_rows)

    @pl.when(has_prev)
    def _():
        e_halo[1].start()
        e_halo[2].start()

    def short_grad(c, ls):
        for i in range(3):
            g_rows = ge[i, pl.ds(0, rows), ls] * scale
            for j in range(short):
                ssend[c, pl.ds(i * EDGE + j, 1), :] = jnp.sum(
                    g_rows * xe[i, pl.ds(EDGE - j, rows), ls], axis=0, keepdims=True
                )
            for j in range(short, EDGE):
                ssend[c, pl.ds(i * EDGE + j, 1), :] = jnp.zeros((1, LANES), F32)
    over(LANES, short_grad)
    to_owners(*short_set[:4])

    owner_sum(*medium_set)

    @pl.when(has_next)
    def _():
        for i in range(3):
            e_halo[i].wait_recv()

    outs = (gq_ref, gk_ref, gv_ref)

    def feature_grad(c, ls):
        for i in range(3):
            total = sf[i, pl.ds(0, 1), ls] * ge[i, pl.ds(0, rows), ls]
            for j in range(1, short):
                total = total + sf[i, pl.ds(j, 1), ls] * ge[i, pl.ds(j, rows), ls]
            outs[i][:, ls] = total
    over(LANES, feature_grad)

    owner_sum(*short_set)
    out_ref[...] = add_sums(0, 0, bits)

    from_owners(mall, ma_ss, ma_rs)
    from_owners(sall, sa_ss, sa_rs)

    for o in range(n_own):
        columns = slice(o * LANES, (o + 1) * LANES)
        gm_ref[:, columns] = mall[o]
        for i in range(3):
            gs_ref[i, :, columns] = sall[o, i * EDGE:i * EDGE + short]

    end_sends(*medium_set)
    end_sends(*short_set)
    for r in range(1, n_tile):
        gather[r].wait_send()
        scatter[r].wait_send()

    @pl.when(has_next)
    def _():
        for i in range(3):
            x_halo[i].wait_send()
        ghalo.wait_send()

    @pl.when(has_prev)
    def _():
        for i in range(3):
            e_halo[i].wait_send()
        mhalo.wait_send()


def shards(n_seq, n_tile, query_feat, key_feat, value_feat, short_filter, medium_filter, out_weight, cotangent):
    rows, width = query_feat.shape
    short = short_filter.shape[1]
    taps = medium_filter.shape[0]
    block = cotangent.shape[1]
    size = rows + taps
    n_own = width // LANES
    assert n_own <= n_seq and short <= EDGE and rows >= taps
    scale = 1.0 / math.sqrt(n_seq * rows)
    consts = dft_consts(rows, taps)
    big = jax.ShapeDtypeStruct((rows, width), F32)
    hbm = pl.BlockSpec(memory_space=pl.ANY)
    vmem = pl.BlockSpec(memory_space=pltpu.VMEM)
    dma = pltpu.SemaphoreType.DMA
    return pl.pallas_call(
        functools.partial(kernel, n_seq, n_tile, n_own, scale),
        out_shape=(
            jax.ShapeDtypeStruct((rows, block), F32),
            big,
            big,
            big,
            jax.ShapeDtypeStruct(short_filter.shape, F32),
            jax.ShapeDtypeStruct(medium_filter.shape, F32),
        ),
        in_specs=[hbm] * 5 + [vmem] * 9,
        out_specs=[vmem] * 6,
        scratch_shapes=[
            pltpu.VMEM((3, rows + EDGE, width), F32),
            pltpu.VMEM((n_tile, width, block), BF16),
            pltpu.VMEM((n_tile, rows, block), BF16),
            pltpu.VMEM((size, width), F32),
            pltpu.VMEM((size, width), F32),
            pltpu.VMEM((size, width), F32),
            pltpu.VMEM((rows, width), F32),
            pltpu.VMEM((rows, width), F32),
            pltpu.VMEM((rows, width), F32),
            pltpu.VMEM((rows, width), F32),
            pltpu.VMEM((rows, width), F32),
            pltpu.VMEM((rows, width), F32),
            pltpu.VMEM((3, rows + EDGE, width), F32),
            pltpu.VMEM((rows, width), BF16),
            pltpu.VMEM((n_tile, rows, block), F32),
            pltpu.VMEM((taps, width), BF16),
            pltpu.VMEM((taps, width), BF16),
            pltpu.VMEM((taps, width), BF16),
            pltpu.VMEM((taps, width), BF16),
            pltpu.VMEM((n_tile, rows, block), BF16),
            pltpu.VMEM((n_tile, rows, block), BF16),
            pltpu.VMEM((n_own, taps, LANES), F32),
            pltpu.VMEM((n_seq, taps, LANES), F32),
            pltpu.VMEM((n_own, taps, LANES), F32),
            pltpu.VMEM((n_own, 3 * EDGE, LANES), F32),
            pltpu.VMEM((n_seq, 3 * EDGE, LANES), F32),
            pltpu.VMEM((n_own, 3 * EDGE, LANES), F32),
            dma((3,)),
            dma((n_tile,)),
            dma,
            dma((3,)),
            dma((3,)),
            dma((n_tile,)),
            dma((n_tile,)),
            dma,
            dma,
            dma,
            dma,
            dma((3,)),
            dma((3,)),
            dma((n_tile,)),
            dma((n_tile,)),
            *[dma((n_seq,)) for _ in range(8)],
        ],
        compiler_params=pltpu.CompilerParams(
            collective_id=0, has_side_effects=True, vmem_limit_bytes=60 * 1024 * 1024
        ),
    )(
        query_feat, key_feat, value_feat, cotangent, out_weight, short_filter, medium_filter,
        *[jnp.asarray(c) for c in consts],
    )


def solution(mesh):
    in_specs = (
        P("seq", "tile"),
        P("seq", "tile"),
        P("seq", "tile"),
        P(None, None, "tile"),
        P(None, "tile"),
        P("tile", None),
        P("seq", "tile"),
    )
    out_specs = (
        P("seq", "tile"),
        P("seq", "tile"),
        P("seq", "tile"),
        P("seq", "tile"),
        P(None, None, "tile"),
        P(None, "tile"),
    )
    body = functools.partial(shards, mesh.shape["seq"], mesh.shape["tile"])
    return jax.shard_map(body, mesh=mesh, in_specs=in_specs, out_specs=out_specs, check_vma=False)
```

```python
import functools
import math

import jax
import jax.numpy as jnp
import ml_dtypes
import numpy as np
from jax import lax
from jax.experimental import pallas as pl
from jax.experimental.pallas import tpu as pltpu
from jax.sharding import PartitionSpec as P

MESH = pl.DeviceIdType.MESH
F32 = jnp.float32
BF16 = jnp.bfloat16
LANES = 128
WIDE = 256
EDGE = 8


def split_const(matrix):
    hi = matrix.astype(np.float32).astype(ml_dtypes.bfloat16)
    lo = (matrix - hi.astype(np.float64)).astype(np.float32).astype(ml_dtypes.bfloat16)
    return np.stack([hi, lo])


def dft_consts(rows, taps):
    size = rows + taps
    theta = 2.0 * np.pi * (np.arange(size // 2) + 0.5) / size

    def forward(first, last):
        angle = theta[:, None] * np.arange(first, last)[None, :]
        return split_const(np.concatenate([np.cos(angle), -np.sin(angle)], axis=0))

    def inverse(first, last):
        angle = np.arange(first, last)[:, None] * theta[None, :]
        return split_const(np.concatenate([np.cos(angle), -np.sin(angle)], axis=1) * (2.0 / size))

    return (
        forward(0, taps),
        forward(taps, size),
        forward(0, rows),
        forward(rows, size),
        inverse(taps, size),
        inverse(0, rows),
        inverse(-taps, 0),
    )


def mm(a, b):
    return jnp.dot(a, b, preferred_element_type=F32)


def dft_wide(matrix, x):
    hi = x.astype(BF16)
    lo = (x - hi.astype(F32)).astype(BF16)
    return mm(matrix[0], hi) + mm(matrix[1], hi) + mm(matrix[0], lo)


def dft_half(matrix, x):
    return mm(matrix[0], x) + mm(matrix[1], x)


def times(a, b):
    half = a.shape[0] // 2
    ar, ai, br, bi = a[:half], a[half:], b[:half], b[half:]
    return jnp.concatenate([ar * br - ai * bi, ar * bi + ai * br], axis=0)


def conj_times(a, b):
    half = a.shape[0] // 2
    ar, ai, br, bi = a[:half], a[half:], b[:half], b[half:]
    return jnp.concatenate([ar * br + ai * bi, ar * bi - ai * br], axis=0)


def low_bit(r):
    return (r & -r).bit_length() - 1


def kernel(
    n_seq, n_tile, n_own, scale,
    xq, xk, xv, cot, weight, sf, mf, fw_taps, fw_tail, fw_head, fw_after, inv_tail, inv_head, inv_taps,
    out_ref, gq_ref, gk_ref, gv_ref, gs_ref, gm_ref,
    xe, wv, cotv, hspec, gspec, vspec, ks, vs, qs, gated, gg, gmix, ge, gout, part,
    ghalo_s, ghalo_r, mhalo_s, mhalo_r, psend, precv, msend, mrecv, mall, ssend, srecv, sall,
    x_sem, w_sem, c_sem, xh_ss, xh_rs, ca_ss, ca_rs, gh_ss, gh_rs, mh_ss, mh_rs,
    eh_ss, eh_rs, p_ss, p_rs, m_ss, m_rs, ma_ss, ma_rs, s_ss, s_rs, sa_ss, sa_rs,
):
    rows, width = ks.shape
    taps = mf.shape[0]
    short = sf.shape[1]
    block = cotv.shape[2]
    bits = n_tile.bit_length() - 1
    x_refs = (xq, xk, xv)
    me = lax.axis_index("seq")
    tile = lax.axis_index("tile")

    def flip(k):
        return tile + (1 << k) - (2 << k) * ((tile // (1 << k)) % 2)

    def relative(r):
        index = tile * 0
        for k in range(bits):
            bit = (tile // (1 << k)) % 2
            index = index + (1 << k) * ((1 - bit) if (r >> k) & 1 else bit)
        return index

    def to_seq(src, dst, send, recv, index):
        return pltpu.make_async_remote_copy(src, dst, send, recv, device_id={"seq": index}, device_id_type=MESH)

    def to_tile(src, dst, send, recv, k):
        return pltpu.make_async_remote_copy(src, dst, send, recv, device_id={"tile": flip(k)}, device_id_type=MESH)

    def lanes(c, size):
        return pl.ds(pl.multiple_of(c * size, size), size)

    def over(size, body):
        def step(c, carry):
            body(c, lanes(c, size))
            return carry
        lax.fori_loop(0, width // size, step, 0)

    x_copies = [pltpu.make_async_copy(x_refs[i], xe.at[i, pl.ds(EDGE, rows)], x_sem.at[i]) for i in range(3)]
    for copy in x_copies:
        copy.start()
    own_cot = pltpu.make_async_copy(cot, cotv.at[0], c_sem)
    own_cot.start()
    w_copies = []
    for r in range(n_tile):
        columns = pl.ds(pl.multiple_of(relative(r) * block, block), block)
        w_copies.append(pltpu.make_async_copy(weight.at[:, columns], wv.at[r], w_sem.at[r]))
        w_copies[-1].start()

    barrier = pltpu.get_barrier_semaphore()

    def greet(d, carry):
        pl.semaphore_signal(barrier, inc=1, device_id={"seq": (me + d) % n_seq}, device_id_type=MESH)
        return carry
    lax.fori_loop(1, n_seq, greet, 0)
    for k in range(bits):
        pl.semaphore_signal(barrier, inc=1, device_id={"tile": flip(k)}, device_id_type=MESH)
    pl.semaphore_wait(barrier, n_seq - 1 + bits)

    has_next = me < n_seq - 1
    has_prev = me > 0
    nxt = (me + 1) % n_seq
    prv = (me + n_seq - 1) % n_seq

    x_halo = [
        to_seq(x_refs[i].at[pl.ds(rows - EDGE, EDGE)], xe.at[i, pl.ds(0, EDGE)], xh_ss.at[i], xh_rs.at[i], nxt)
        for i in range(3)
    ]

    @pl.when(has_next)
    def _():
        for i in (1, 2, 0):
            x_halo[i].start()

    gather = {}
    for k in reversed(range(bits)):
        gather[1 << k] = to_tile(cot, cotv.at[1 << k], ca_ss.at[1 << k], ca_rs.at[1 << k], k)
        gather[1 << k].start()

    @pl.when(jnp.logical_not(has_prev))
    def _():
        for i in range(3):
            xe[i, pl.ds(0, EDGE), :] = jnp.zeros((EDGE, width), F32)
        ghalo_r[...] = jnp.zeros_like(ghalo_r)

    @pl.when(jnp.logical_not(has_next))
    def _():
        for i in range(3):
            ge[i, pl.ds(rows, EDGE), :] = jnp.zeros((EDGE, width), F32)
        mhalo_r[...] = jnp.zeros_like(mhalo_r)

    def filter_spectrum(c, ls):
        hspec[:, ls] = dft_wide(fw_taps, mf[:, ls])
    over(WIDE, filter_spectrum)

    for copy in x_copies:
        copy.wait()

    @pl.when(has_prev)
    def _():
        for i in range(3):
            x_halo[i].wait_recv()

    def short_conv(i, ls):
        total = sf[i, pl.ds(0, 1), ls] * xe[i, pl.ds(EDGE, rows), ls]
        for j in range(1, short):
            total = total + sf[i, pl.ds(j, 1), ls] * xe[i, pl.ds(EDGE - j, rows), ls]
        return total

    def key_value(c, ls):
        k_rows = short_conv(1, ls)
        ks[:, ls] = k_rows
        v_rows = short_conv(2, ls)
        vs[:, ls] = v_rows
        product = k_rows * v_rows
        gated[:, ls] = product
        ghalo_s[:, ls] = product[rows - taps:].astype(BF16)
    over(LANES, key_value)

    ghalo = to_seq(ghalo_s, ghalo_r, gh_ss, gh_rs, nxt)

    @pl.when(has_next)
    def _():
        ghalo.start()

    def query(c, ls):
        qs[:, ls] = short_conv(0, ls)
    over(LANES, query)

    def gated_spectrum(c, ls):
        gspec[:, ls] = dft_wide(fw_tail, gated[:, ls])
    over(WIDE, gated_spectrum)

    for r in range(n_tile):
        if r == 0:
            own_cot.wait()
        else:
            gather[r].wait_recv()
            for k in reversed(range(low_bit(r))):
                slot = r + (1 << k)
                gather[slot] = to_tile(cotv.at[r], cotv.at[slot], ca_ss.at[slot], ca_rs.at[slot], k)
                gather[slot].start()
        w_copies[r].wait()

        def grad_block(c, ls, r=r):
            term = lax.dot_general(
                cotv[r], wv[r, ls, :], (((1,), (1,)), ((), ())), preferred_element_type=F32
            )
            if r > 0:
                term = term + gg[:, ls]
            gg[:, ls] = term
            if r == n_tile - 1:
                grad_mixed = term * qs[:, ls]
                gmix[:, ls] = grad_mixed
                mhalo_s[:, ls] = grad_mixed[:taps].astype(BF16)
        over(WIDE, grad_block)

    mhalo = to_seq(mhalo_s, mhalo_r, mh_ss, mh_rs, prv)

    @pl.when(has_prev)
    def _():
        mhalo.start()

    @pl.when(has_prev)
    def _():
        ghalo.wait_recv()

    def mixed_rows(c, ls):
        spectrum = gspec[:, ls] + dft_half(fw_taps, ghalo_r[:, ls])
        gspec[:, ls] = spectrum
        mixed = dft_wide(inv_tail, times(spectrum, hspec[:, ls]))
        gout[:, ls] = (qs[:, ls] * mixed).astype(BF16)
        ge[0, pl.ds(0, rows), ls] = gg[:, ls] * mixed
    over(WIDE, mixed_rows)

    e_halo = [
        to_seq(ge.at[i, pl.ds(0, EDGE)], ge.at[i, pl.ds(rows, EDGE)], eh_ss.at[i], eh_rs.at[i], prv) for i in range(3)
    ]

    @pl.when(has_prev)
    def _():
        e_halo[0].start()

    scatter = {}

    def project(r):
        def body(c, carry):
            ds = lanes(c, WIDE)
            term = mm(gout[...], wv[r, :, ds])
            if r & 1:
                psend[r, :, ds] = term.astype(BF16)
            else:
                part[r, :, ds] = term
            return carry
        lax.fori_loop(0, block // WIDE, body, 0)

    def send_sum(r):
        k = low_bit(r)
        scatter[r] = to_tile(psend.at[r], precv.at[r], p_ss.at[r], p_rs.at[r], k)
        scatter[r].start()

    per_wide = WIDE // LANES

    def medium_grad(c, ls):
        v_spec = dft_wide(fw_head, gmix[:, ls])
        vspec[:, ls] = v_spec
        terms = dft_wide(inv_taps, conj_times(gspec[:, ls], v_spec)) * scale
        for p in range(per_wide):
            msend[c * per_wide + p] = terms[:, p * LANES:(p + 1) * LANES].astype(BF16)
    over(WIDE, medium_grad)

    def owner_copy(send, recv, ss, rs, d):
        return to_seq(send.at[(me + d) % n_seq], recv.at[d], ss.at[d], rs.at[d], (me + d) % n_seq)

    def if_owner(index, body):
        if n_own == n_seq:
            body()
        else:
            pl.when(index < n_own)(body)

    def peers(body):
        def step(d, carry):
            body(d)
            return carry
        lax.fori_loop(1, n_seq, step, 0)

    def to_owners(send, recv, ss, rs):
        peers(lambda d: if_owner((me + d) % n_seq, lambda: owner_copy(send, recv, ss, rs, d).start()))

    def from_owner_copy(full, ss, rs, d):
        return to_seq(full.at[me], full.at[me], ss.at[d], rs.at[d], (me + d) % n_seq)

    def owner_sum(send, recv, ss, rs, full, f_ss, f_rs):
        def body():
            def add(d, total):
                owner_copy(send, recv, ss, rs, d).wait_recv()
                return total + recv[d].astype(F32)
            total = lax.fori_loop(1, n_seq, add, send[me].astype(F32))
            full[me] = total.astype(full.dtype)
            peers(lambda d: from_owner_copy(full, f_ss, f_rs, d).start())
        if_owner(me, body)

    def from_owners(full, ss, rs):
        def wait(d):
            source = (me + n_seq - d) % n_seq
            if_owner(source, lambda: to_seq(full.at[source], full.at[source], ss.at[d], rs.at[d], source).wait_recv())
        peers(wait)

    def end_sends(send, recv, ss, rs, full, f_ss, f_rs):
        peers(lambda d: if_owner((me + d) % n_seq, lambda: owner_copy(send, recv, ss, rs, d).wait_send()))
        if_owner(me, lambda: peers(lambda d: from_owner_copy(full, f_ss, f_rs, d).wait_send()))

    medium_set = (msend, mrecv, m_ss, m_rs, mall, ma_ss, ma_rs)
    short_set = (ssend, srecv, s_ss, s_rs, sall, sa_ss, sa_rs)
    to_owners(*medium_set[:4])

    for r in sorted(range(n_tile), key=lambda r: (1 - (r & 1), -r)):
        project(r)
        if r & 1:
            send_sum(r)

    def add_sums(r, first, last):
        total = part[r]
        for k in range(first, last):
            scatter[r + (1 << k)].wait_recv()
            total = total + precv[r + (1 << k)].astype(F32)
        return total

    def step_sums(k):
        for r in range(1 << k, n_tile, 2 << k):
            psend[r] = add_sums(r, 0, k).astype(BF16)
            send_sum(r)

    for k in range(1, bits):
        step_sums(k)

    @pl.when(has_next)
    def _():
        mhalo.wait_recv()

    def product_rows(c, ls):
        spectrum = vspec[:, ls] + dft_half(fw_after, mhalo_r[:, ls])
        grad_prod = dft_wide(inv_head, conj_times(hspec[:, ls], spectrum))
        ge[1, pl.ds(0, rows), ls] = grad_prod * vs[:, ls]
        ge[2, pl.ds(0, rows), ls] = grad_prod * ks[:, ls]
    over(WIDE, product_rows)

    @pl.when(has_prev)
    def _():
        e_halo[1].start()
        e_halo[2].start()

    def short_grad(c, ls):
        for i in range(3):
            g_rows = ge[i, pl.ds(0, rows), ls] * scale
            for j in range(short):
                ssend[c, pl.ds(i * EDGE + j, 1), :] = jnp.sum(
                    g_rows * xe[i, pl.ds(EDGE - j, rows), ls], axis=0, keepdims=True
                )
            for j in range(short, EDGE):
                ssend[c, pl.ds(i * EDGE + j, 1), :] = jnp.zeros((1, LANES), F32)
    over(LANES, short_grad)
    to_owners(*short_set[:4])

    owner_sum(*medium_set)

    @pl.when(has_next)
    def _():
        for i in range(3):
            e_halo[i].wait_recv()

    outs = (gq_ref, gk_ref, gv_ref)

    def feature_grad(c, ls):
        for i in range(3):
            total = sf[i, pl.ds(0, 1), ls] * ge[i, pl.ds(0, rows), ls]
            for j in range(1, short):
                total = total + sf[i, pl.ds(j, 1), ls] * ge[i, pl.ds(j, rows), ls]
            outs[i][:, ls] = total
    over(LANES, feature_grad)

    owner_sum(*short_set)
    out_ref[...] = add_sums(0, 0, bits)

    from_owners(mall, ma_ss, ma_rs)
    from_owners(sall, sa_ss, sa_rs)

    for o in range(n_own):
        columns = slice(o * LANES, (o + 1) * LANES)
        gm_ref[:, columns] = mall[o].astype(F32)
        for i in range(3):
            gs_ref[i, :, columns] = sall[o, i * EDGE:i * EDGE + short]

    end_sends(*medium_set)
    end_sends(*short_set)
    for r in range(1, n_tile):
        gather[r].wait_send()
        scatter[r].wait_send()

    @pl.when(has_next)
    def _():
        for i in range(3):
            x_halo[i].wait_send()
        ghalo.wait_send()

    @pl.when(has_prev)
    def _():
        for i in range(3):
            e_halo[i].wait_send()
        mhalo.wait_send()


def write_results(*refs):
    count = len(refs) // 2
    sems = refs[-1]
    copies = [pltpu.make_async_copy(refs[i], refs[count + i], sems.at[i]) for i in range(count)]
    for copy in copies:
        copy.start()
    for copy in copies:
        copy.wait()


def shards(n_seq, n_tile, query_feat, key_feat, value_feat, short_filter, medium_filter, out_weight, cotangent):
    rows, width = query_feat.shape
    short = short_filter.shape[1]
    taps = medium_filter.shape[0]
    block = cotangent.shape[1]
    size = rows + taps
    n_own = width // LANES
    assert n_own <= n_seq and short <= EDGE and rows >= taps
    scale = 1.0 / math.sqrt(n_seq * rows)
    consts = dft_consts(rows, taps)
    big = jax.ShapeDtypeStruct((rows, width), F32)
    hbm = pl.BlockSpec(memory_space=pl.ANY)
    vmem = pl.BlockSpec(memory_space=pltpu.VMEM)
    dma = pltpu.SemaphoreType.DMA
    results = pl.pallas_call(
        functools.partial(kernel, n_seq, n_tile, n_own, scale),
        out_shape=(
            jax.ShapeDtypeStruct((rows, block), F32),
            big,
            big,
            big,
            jax.ShapeDtypeStruct(short_filter.shape, F32),
            jax.ShapeDtypeStruct(medium_filter.shape, F32),
        ),
        in_specs=[hbm] * 5 + [vmem] * 9,
        out_specs=[vmem] * 6,
        scratch_shapes=[
            pltpu.VMEM((3, rows + EDGE, width), F32),
            pltpu.VMEM((n_tile, width, block), BF16),
            pltpu.VMEM((n_tile, rows, block), BF16),
            pltpu.VMEM((size, width), F32),
            pltpu.VMEM((size, width), F32),
            pltpu.VMEM((size, width), F32),
            pltpu.VMEM((rows, width), F32),
            pltpu.VMEM((rows, width), F32),
            pltpu.VMEM((rows, width), F32),
            pltpu.VMEM((rows, width), F32),
            pltpu.VMEM((rows, width), F32),
            pltpu.VMEM((rows, width), F32),
            pltpu.VMEM((3, rows + EDGE, width), F32),
            pltpu.VMEM((rows, width), BF16),
            pltpu.VMEM((n_tile, rows, block), F32),
            pltpu.VMEM((taps, width), BF16),
            pltpu.VMEM((taps, width), BF16),
            pltpu.VMEM((taps, width), BF16),
            pltpu.VMEM((taps, width), BF16),
            pltpu.VMEM((n_tile, rows, block), BF16),
            pltpu.VMEM((n_tile, rows, block), BF16),
            pltpu.VMEM((n_own, taps, LANES), BF16),
            pltpu.VMEM((n_seq, taps, LANES), BF16),
            pltpu.VMEM((n_own, taps, LANES), BF16),
            pltpu.VMEM((n_own, 3 * EDGE, LANES), F32),
            pltpu.VMEM((n_seq, 3 * EDGE, LANES), F32),
            pltpu.VMEM((n_own, 3 * EDGE, LANES), F32),
            dma((3,)),
            dma((n_tile,)),
            dma,
            dma((3,)),
            dma((3,)),
            dma((n_tile,)),
            dma((n_tile,)),
            dma,
            dma,
            dma,
            dma,
            dma((3,)),
            dma((3,)),
            dma((n_tile,)),
            dma((n_tile,)),
            *[dma((n_seq,)) for _ in range(8)],
        ],
        compiler_params=pltpu.CompilerParams(
            collective_id=0, has_side_effects=True, vmem_limit_bytes=48 * 1024 * 1024
        ),
    )(
        query_feat, key_feat, value_feat, cotangent, out_weight, short_filter, medium_filter,
        *[jnp.asarray(c) for c in consts],
    )
    return pl.pallas_call(
        write_results,
        out_shape=tuple(jax.ShapeDtypeStruct(r.shape, r.dtype) for r in results),
        in_specs=[hbm] * len(results),
        out_specs=[hbm] * len(results),
        scratch_shapes=[dma((len(results),))],
    )(*results)


def solution(mesh):
    in_specs = (
        P("seq", "tile"),
        P("seq", "tile"),
        P("seq", "tile"),
        P(None, None, "tile"),
        P(None, "tile"),
        P("tile", None),
        P("seq", "tile"),
    )
    out_specs = (
        P("seq", "tile"),
        P("seq", "tile"),
        P("seq", "tile"),
        P("seq", "tile"),
        P(None, None, "tile"),
        P(None, "tile"),
    )
    body = functools.partial(shards, mesh.shape["seq"], mesh.shape["tile"])
    return jax.shard_map(body, mesh=mesh, in_specs=in_specs, out_specs=out_specs, check_vma=False)
```

```python
import functools
import math

import jax
import jax.numpy as jnp
import ml_dtypes
import numpy as np
from jax import lax
from jax.experimental import pallas as pl
from jax.experimental.pallas import tpu as pltpu
from jax.sharding import PartitionSpec as P

MESH = pl.DeviceIdType.MESH
F32 = jnp.float32
BF16 = jnp.bfloat16
LANES = 128
WIDE = 256
EDGE = 8


def split_const(matrix):
    hi = matrix.astype(np.float32).astype(ml_dtypes.bfloat16)
    lo = (matrix - hi.astype(np.float64)).astype(np.float32).astype(ml_dtypes.bfloat16)
    return np.stack([hi, lo])


def dft_consts(rows, taps):
    size = rows + taps
    theta = 2.0 * np.pi * (np.arange(size // 2) + 0.5) / size

    def forward(first, last):
        angle = theta[:, None] * np.arange(first, last)[None, :]
        return split_const(np.concatenate([np.cos(angle), -np.sin(angle)], axis=0))

    def inverse(first, last):
        angle = np.arange(first, last)[:, None] * theta[None, :]
        return split_const(np.concatenate([np.cos(angle), -np.sin(angle)], axis=1) * (2.0 / size))

    return (
        forward(0, taps),
        forward(taps, size),
        forward(0, rows),
        forward(rows, size),
        inverse(taps, size),
        inverse(0, rows),
        inverse(-taps, 0),
    )


def mm(a, b):
    return jnp.dot(a, b, preferred_element_type=F32)


def dft_wide(matrix, x):
    hi = x.astype(BF16)
    lo = (x - hi.astype(F32)).astype(BF16)
    return mm(matrix[0], hi) + mm(matrix[1], hi) + mm(matrix[0], lo)


def dft_half(matrix, x):
    return mm(matrix[0], x) + mm(matrix[1], x)


def times(a, b):
    half = a.shape[0] // 2
    ar, ai, br, bi = a[:half], a[half:], b[:half], b[half:]
    return jnp.concatenate([ar * br - ai * bi, ar * bi + ai * br], axis=0)


def conj_times(a, b):
    half = a.shape[0] // 2
    ar, ai, br, bi = a[:half], a[half:], b[:half], b[half:]
    return jnp.concatenate([ar * br + ai * bi, ar * bi - ai * br], axis=0)


def low_bit(r):
    return (r & -r).bit_length() - 1


def kernel(
    n_seq, n_tile, n_own, scale,
    xq, xk, xv, cot, weight, sf_in, mf_in, fw_taps_in, fw_tail_in, fw_head_in, fw_after_in, inv_tail_in,
    inv_head_in, inv_taps_in,
    out_ref, gq_ref, gk_ref, gv_ref, gs_ref, gm_ref,
    sf, mf, fw_taps, fw_tail, fw_head, fw_after, inv_tail, inv_head, inv_taps,
    xe, wv, cotv, hspec, gspec, vspec, ks, vs, qs, gated, gg, gmix, ge, gout, part,
    ghalo_s, ghalo_r, mhalo_s, mhalo_r, psend, precv, msend, mrecv, mall, ssend, srecv, sall,
    t_sem, x_sem, w_sem, c_sem, xh_ss, xh_rs, ca_ss, ca_rs, gh_ss, gh_rs, mh_ss, mh_rs,
    eh_ss, eh_rs, p_ss, p_rs, m_ss, m_rs, ma_ss, ma_rs, s_ss, s_rs, sa_ss, sa_rs,
):
    rows, width = ks.shape
    taps = mf.shape[0]
    short = sf.shape[1]
    block = cotv.shape[2]
    bits = n_tile.bit_length() - 1
    x_refs = (xq, xk, xv)
    me = lax.axis_index("seq")
    tile = lax.axis_index("tile")

    def flip(k):
        return tile + (1 << k) - (2 << k) * ((tile // (1 << k)) % 2)

    def relative(r):
        index = tile * 0
        for k in range(bits):
            bit = (tile // (1 << k)) % 2
            index = index + (1 << k) * ((1 - bit) if (r >> k) & 1 else bit)
        return index

    def to_seq(src, dst, send, recv, index):
        return pltpu.make_async_remote_copy(src, dst, send, recv, device_id={"seq": index}, device_id_type=MESH)

    def to_tile(src, dst, send, recv, k):
        return pltpu.make_async_remote_copy(src, dst, send, recv, device_id={"tile": flip(k)}, device_id_type=MESH)

    def lanes(c, size):
        return pl.ds(pl.multiple_of(c * size, size), size)

    def over(size, body):
        def step(c, carry):
            body(c, lanes(c, size))
            return carry
        lax.fori_loop(0, width // size, step, 0)

    table_pairs = (
        (mf_in, mf), (fw_taps_in, fw_taps), (sf_in, sf), (fw_tail_in, fw_tail), (fw_head_in, fw_head),
        (fw_after_in, fw_after), (inv_tail_in, inv_tail), (inv_head_in, inv_head), (inv_taps_in, inv_taps),
    )
    tables = [pltpu.make_async_copy(pair[0], pair[1], t_sem.at[i]) for i, pair in enumerate(table_pairs)]
    for copy in tables[:3]:
        copy.start()
    x_copies = [pltpu.make_async_copy(x_refs[i], xe.at[i, pl.ds(EDGE, rows)], x_sem.at[i]) for i in range(3)]
    for copy in x_copies:
        copy.start()
    own_cot = pltpu.make_async_copy(cot, cotv.at[0], c_sem)
    own_cot.start()
    for copy in tables[3:]:
        copy.start()
    w_copies = []
    for r in range(n_tile):
        columns = pl.ds(pl.multiple_of(relative(r) * block, block), block)
        w_copies.append(pltpu.make_async_copy(weight.at[:, columns], wv.at[r], w_sem.at[r]))
        w_copies[-1].start()

    barrier = pltpu.get_barrier_semaphore()

    def greet(d, carry):
        pl.semaphore_signal(barrier, inc=1, device_id={"seq": (me + d) % n_seq}, device_id_type=MESH)
        return carry
    lax.fori_loop(1, n_seq, greet, 0)
    for k in range(bits):
        pl.semaphore_signal(barrier, inc=1, device_id={"tile": flip(k)}, device_id_type=MESH)
    pl.semaphore_wait(barrier, n_seq - 1 + bits)

    has_next = me < n_seq - 1
    has_prev = me > 0
    nxt = (me + 1) % n_seq
    prv = (me + n_seq - 1) % n_seq

    x_halo = [
        to_seq(x_refs[i].at[pl.ds(rows - EDGE, EDGE)], xe.at[i, pl.ds(0, EDGE)], xh_ss.at[i], xh_rs.at[i], nxt)
        for i in range(3)
    ]

    @pl.when(has_next)
    def _():
        for i in (1, 2, 0):
            x_halo[i].start()

    gather = {}
    for k in reversed(range(bits)):
        gather[1 << k] = to_tile(cot, cotv.at[1 << k], ca_ss.at[1 << k], ca_rs.at[1 << k], k)
        gather[1 << k].start()

    @pl.when(jnp.logical_not(has_prev))
    def _():
        for i in range(3):
            xe[i, pl.ds(0, EDGE), :] = jnp.zeros((EDGE, width), F32)
        ghalo_r[...] = jnp.zeros_like(ghalo_r)

    @pl.when(jnp.logical_not(has_next))
    def _():
        for i in range(3):
            ge[i, pl.ds(rows, EDGE), :] = jnp.zeros((EDGE, width), F32)
        mhalo_r[...] = jnp.zeros_like(mhalo_r)

    for copy in tables[:3]:
        copy.wait()

    def filter_spectrum(c, ls):
        hspec[:, ls] = dft_wide(fw_taps, mf[:, ls])
    over(WIDE, filter_spectrum)

    for copy in x_copies:
        copy.wait()

    @pl.when(has_prev)
    def _():
        for i in range(3):
            x_halo[i].wait_recv()

    def short_conv(i, ls):
        total = sf[i, pl.ds(0, 1), ls] * xe[i, pl.ds(EDGE, rows), ls]
        for j in range(1, short):
            total = total + sf[i, pl.ds(j, 1), ls] * xe[i, pl.ds(EDGE - j, rows), ls]
        return total

    def key_value(c, ls):
        k_rows = short_conv(1, ls)
        ks[:, ls] = k_rows
        v_rows = short_conv(2, ls)
        vs[:, ls] = v_rows
        product = k_rows * v_rows
        gated[:, ls] = product
        ghalo_s[:, ls] = product[rows - taps:].astype(BF16)
    over(LANES, key_value)

    ghalo = to_seq(ghalo_s, ghalo_r, gh_ss, gh_rs, nxt)

    @pl.when(has_next)
    def _():
        ghalo.start()

    def query(c, ls):
        qs[:, ls] = short_conv(0, ls)
    over(LANES, query)

    for copy in tables[3:]:
        copy.wait()

    def gated_spectrum(c, ls):
        gspec[:, ls] = dft_wide(fw_tail, gated[:, ls])
    over(WIDE, gated_spectrum)

    for r in range(n_tile):
        if r == 0:
            own_cot.wait()
        else:
            gather[r].wait_recv()
            for k in reversed(range(low_bit(r))):
                slot = r + (1 << k)
                gather[slot] = to_tile(cotv.at[r], cotv.at[slot], ca_ss.at[slot], ca_rs.at[slot], k)
                gather[slot].start()
        w_copies[r].wait()

        def grad_block(c, ls, r=r):
            term = lax.dot_general(
                cotv[r], wv[r, ls, :], (((1,), (1,)), ((), ())), preferred_element_type=F32
            )
            if r > 0:
                term = term + gg[:, ls]
            gg[:, ls] = term
            if r == n_tile - 1:
                grad_mixed = term * qs[:, ls]
                gmix[:, ls] = grad_mixed
                mhalo_s[:, ls] = grad_mixed[:taps].astype(BF16)
        over(WIDE, grad_block)

    mhalo = to_seq(mhalo_s, mhalo_r, mh_ss, mh_rs, prv)

    @pl.when(has_prev)
    def _():
        mhalo.start()

    @pl.when(has_prev)
    def _():
        ghalo.wait_recv()

    def mixed_rows(c, ls):
        spectrum = gspec[:, ls] + dft_half(fw_taps, ghalo_r[:, ls])
        gspec[:, ls] = spectrum
        mixed = dft_wide(inv_tail, times(spectrum, hspec[:, ls]))
        gout[:, ls] = (qs[:, ls] * mixed).astype(BF16)
        ge[0, pl.ds(0, rows), ls] = gg[:, ls] * mixed
    over(WIDE, mixed_rows)

    e_halo = [
        to_seq(ge.at[i, pl.ds(0, EDGE)], ge.at[i, pl.ds(rows, EDGE)], eh_ss.at[i], eh_rs.at[i], prv) for i in range(3)
    ]

    @pl.when(has_prev)
    def _():
        e_halo[0].start()

    scatter = {}

    def project(r):
        def body(c, carry):
            ds = lanes(c, WIDE)
            term = mm(gout[...], wv[r, :, ds])
            if r & 1:
                psend[r, :, ds] = term.astype(BF16)
            else:
                part[r, :, ds] = term
            return carry
        lax.fori_loop(0, block // WIDE, body, 0)

    def send_sum(r):
        k = low_bit(r)
        scatter[r] = to_tile(psend.at[r], precv.at[r], p_ss.at[r], p_rs.at[r], k)
        scatter[r].start()

    per_wide = WIDE // LANES

    def medium_grad(c, ls):
        v_spec = dft_wide(fw_head, gmix[:, ls])
        vspec[:, ls] = v_spec
        terms = dft_wide(inv_taps, conj_times(gspec[:, ls], v_spec)) * scale
        for p in range(per_wide):
            msend[c * per_wide + p] = terms[:, p * LANES:(p + 1) * LANES].astype(BF16)
    over(WIDE, medium_grad)

    def owner_copy(send, recv, ss, rs, d):
        return to_seq(send.at[(me + d) % n_seq], recv.at[d], ss.at[d], rs.at[d], (me + d) % n_seq)

    def if_owner(index, body):
        if n_own == n_seq:
            body()
        else:
            pl.when(index < n_own)(body)

    def peers(body):
        def step(d, carry):
            body(d)
            return carry
        lax.fori_loop(1, n_seq, step, 0)

    def to_owners(send, recv, ss, rs):
        peers(lambda d: if_owner((me + d) % n_seq, lambda: owner_copy(send, recv, ss, rs, d).start()))

    def from_owner_copy(full, ss, rs, d):
        return to_seq(full.at[me], full.at[me], ss.at[d], rs.at[d], (me + d) % n_seq)

    def owner_sum(send, recv, ss, rs, full, f_ss, f_rs):
        def body():
            def add(d, total):
                owner_copy(send, recv, ss, rs, d).wait_recv()
                return total + recv[d].astype(F32)
            total = lax.fori_loop(1, n_seq, add, send[me].astype(F32))
            full[me] = total.astype(full.dtype)
            peers(lambda d: from_owner_copy(full, f_ss, f_rs, d).start())
        if_owner(me, body)

    def from_owners(full, ss, rs):
        def wait(d):
            source = (me + n_seq - d) % n_seq
            if_owner(source, lambda: to_seq(full.at[source], full.at[source], ss.at[d], rs.at[d], source).wait_recv())
        peers(wait)

    def end_sends(send, recv, ss, rs, full, f_ss, f_rs):
        peers(lambda d: if_owner((me + d) % n_seq, lambda: owner_copy(send, recv, ss, rs, d).wait_send()))
        if_owner(me, lambda: peers(lambda d: from_owner_copy(full, f_ss, f_rs, d).wait_send()))

    medium_set = (msend, mrecv, m_ss, m_rs, mall, ma_ss, ma_rs)
    short_set = (ssend, srecv, s_ss, s_rs, sall, sa_ss, sa_rs)
    to_owners(*medium_set[:4])

    for r in sorted(range(n_tile), key=lambda r: (1 - (r & 1), -r)):
        project(r)
        if r & 1:
            send_sum(r)

    def add_sums(r, first, last):
        total = part[r]
        for k in range(first, last):
            scatter[r + (1 << k)].wait_recv()
            total = total + precv[r + (1 << k)].astype(F32)
        return total

    def step_sums(k):
        for r in range(1 << k, n_tile, 2 << k):
            psend[r] = add_sums(r, 0, k).astype(BF16)
            send_sum(r)

    for k in range(1, bits):
        step_sums(k)

    @pl.when(has_next)
    def _():
        mhalo.wait_recv()

    def product_rows(c, ls):
        spectrum = vspec[:, ls] + dft_half(fw_after, mhalo_r[:, ls])
        grad_prod = dft_wide(inv_head, conj_times(hspec[:, ls], spectrum))
        ge[1, pl.ds(0, rows), ls] = grad_prod * vs[:, ls]
        ge[2, pl.ds(0, rows), ls] = grad_prod * ks[:, ls]
    over(WIDE, product_rows)

    @pl.when(has_prev)
    def _():
        e_halo[1].start()
        e_halo[2].start()

    def short_grad(c, ls):
        for i in range(3):
            g_rows = ge[i, pl.ds(0, rows), ls] * scale
            for j in range(short):
                ssend[c, pl.ds(i * EDGE + j, 1), :] = jnp.sum(
                    g_rows * xe[i, pl.ds(EDGE - j, rows), ls], axis=0, keepdims=True
                )
            for j in range(short, EDGE):
                ssend[c, pl.ds(i * EDGE + j, 1), :] = jnp.zeros((1, LANES), F32)
    over(LANES, short_grad)
    to_owners(*short_set[:4])

    owner_sum(*medium_set)

    @pl.when(has_next)
    def _():
        for i in range(3):
            e_halo[i].wait_recv()

    outs = (gq_ref, gk_ref, gv_ref)

    def feature_grad(c, ls):
        for i in range(3):
            total = sf[i, pl.ds(0, 1), ls] * ge[i, pl.ds(0, rows), ls]
            for j in range(1, short):
                total = total + sf[i, pl.ds(j, 1), ls] * ge[i, pl.ds(j, rows), ls]
            outs[i][:, ls] = total
    over(LANES, feature_grad)

    owner_sum(*short_set)
    out_ref[...] = add_sums(0, 0, bits)

    from_owners(mall, ma_ss, ma_rs)
    from_owners(sall, sa_ss, sa_rs)

    for o in range(n_own):
        columns = slice(o * LANES, (o + 1) * LANES)
        gm_ref[:, columns] = mall[o].astype(F32)
        for i in range(3):
            gs_ref[i, :, columns] = sall[o, i * EDGE:i * EDGE + short]

    end_sends(*medium_set)
    end_sends(*short_set)
    for r in range(1, n_tile):
        gather[r].wait_send()
        scatter[r].wait_send()

    @pl.when(has_next)
    def _():
        for i in range(3):
            x_halo[i].wait_send()
        ghalo.wait_send()

    @pl.when(has_prev)
    def _():
        for i in range(3):
            e_halo[i].wait_send()
        mhalo.wait_send()


def write_results(*refs):
    count = len(refs) // 2
    sems = refs[-1]
    copies = [pltpu.make_async_copy(refs[i], refs[count + i], sems.at[i]) for i in range(count)]
    for copy in copies:
        copy.start()
    for copy in copies:
        copy.wait()


def shards(n_seq, n_tile, query_feat, key_feat, value_feat, short_filter, medium_filter, out_weight, cotangent):
    rows, width = query_feat.shape
    short = short_filter.shape[1]
    taps = medium_filter.shape[0]
    block = cotangent.shape[1]
    size = rows + taps
    n_own = width // LANES
    assert n_own <= n_seq and short <= EDGE and rows >= taps
    scale = 1.0 / math.sqrt(n_seq * rows)
    consts = dft_consts(rows, taps)
    hbm = pl.BlockSpec(memory_space=pltpu.HBM)
    vmem = pl.BlockSpec(memory_space=pltpu.VMEM)
    dma = pltpu.SemaphoreType.DMA
    results = pl.pallas_call(
        functools.partial(kernel, n_seq, n_tile, n_own, scale),
        out_shape=(
            pltpu.VMEM((rows, block), F32),
            pltpu.VMEM((rows, width), F32),
            pltpu.VMEM((rows, width), F32),
            pltpu.VMEM((rows, width), F32),
            pltpu.VMEM(short_filter.shape, F32),
            pltpu.VMEM(medium_filter.shape, F32),
        ),
        in_specs=[hbm] * 14,
        out_specs=[vmem] * 6,
        scratch_shapes=[
            pltpu.VMEM(short_filter.shape, F32),
            pltpu.VMEM(medium_filter.shape, F32),
            *[pltpu.VMEM(c.shape, BF16) for c in consts],
            pltpu.VMEM((3, rows + EDGE, width), F32),
            pltpu.VMEM((n_tile, width, block), BF16),
            pltpu.VMEM((n_tile, rows, block), BF16),
            pltpu.VMEM((size, width), F32),
            pltpu.VMEM((size, width), F32),
            pltpu.VMEM((size, width), F32),
            pltpu.VMEM((rows, width), F32),
            pltpu.VMEM((rows, width), F32),
            pltpu.VMEM((rows, width), F32),
            pltpu.VMEM((rows, width), F32),
            pltpu.VMEM((rows, width), F32),
            pltpu.VMEM((rows, width), F32),
            pltpu.VMEM((3, rows + EDGE, width), F32),
            pltpu.VMEM((rows, width), BF16),
            pltpu.VMEM((n_tile, rows, block), F32),
            pltpu.VMEM((taps, width), BF16),
            pltpu.VMEM((taps, width), BF16),
            pltpu.VMEM((taps, width), BF16),
            pltpu.VMEM((taps, width), BF16),
            pltpu.VMEM((n_tile, rows, block), BF16),
            pltpu.VMEM((n_tile, rows, block), BF16),
            pltpu.VMEM((n_own, taps, LANES), BF16),
            pltpu.VMEM((n_seq, taps, LANES), BF16),
            pltpu.VMEM((n_own, taps, LANES), BF16),
            pltpu.VMEM((n_own, 3 * EDGE, LANES), F32),
            pltpu.VMEM((n_seq, 3 * EDGE, LANES), F32),
            pltpu.VMEM((n_own, 3 * EDGE, LANES), F32),
            dma((9,)),
            dma((3,)),
            dma((n_tile,)),
            dma,
            dma((3,)),
            dma((3,)),
            dma((n_tile,)),
            dma((n_tile,)),
            dma,
            dma,
            dma,
            dma,
            dma((3,)),
            dma((3,)),
            dma((n_tile,)),
            dma((n_tile,)),
            *[dma((n_seq,)) for _ in range(8)],
        ],
        compiler_params=pltpu.CompilerParams(
            collective_id=0, has_side_effects=True, vmem_limit_bytes=50 * 1024 * 1024
        ),
    )(
        query_feat, key_feat, value_feat, cotangent, out_weight, short_filter, medium_filter,
        *[jnp.asarray(c) for c in consts],
    )
    return pl.pallas_call(
        write_results,
        out_shape=tuple(jax.ShapeDtypeStruct(r.shape, r.dtype) for r in results),
        in_specs=[vmem] * len(results),
        out_specs=[hbm] * len(results),
        scratch_shapes=[dma((len(results),))],
    )(*results)


def solution(mesh):
    in_specs = (
        P("seq", "tile"),
        P("seq", "tile"),
        P("seq", "tile"),
        P(None, None, "tile"),
        P(None, "tile"),
        P("tile", None),
        P("seq", "tile"),
    )
    out_specs = (
        P("seq", "tile"),
        P("seq", "tile"),
        P("seq", "tile"),
        P("seq", "tile"),
        P(None, None, "tile"),
        P(None, "tile"),
    )
    body = functools.partial(shards, mesh.shape["seq"], mesh.shape["tile"])
    return jax.shard_map(body, mesh=mesh, in_specs=in_specs, out_specs=out_specs, check_vma=False)
```

```python
import functools
import math

import jax
import jax.numpy as jnp
import ml_dtypes
import numpy as np
from jax import lax
from jax.experimental import pallas as pl
from jax.experimental.pallas import tpu as pltpu
from jax.sharding import PartitionSpec as P

MESH = pl.DeviceIdType.MESH
F32 = jnp.float32
BF16 = jnp.bfloat16
LANES = 128
WIDE = 256
EDGE = 8


def split_const(matrix, wide=True):
    hi = matrix.astype(np.float32).astype(ml_dtypes.bfloat16)
    lo = (matrix - hi.astype(np.float64)).astype(np.float32).astype(ml_dtypes.bfloat16)
    return np.concatenate([hi, lo, hi] if wide else [hi, lo], axis=1)


def dft_consts(rows, taps):
    size = rows + taps
    theta = 2.0 * np.pi * (np.arange(size // 2) + 0.5) / size

    def forward(first, last, wide=True):
        angle = theta[:, None] * np.arange(first, last)[None, :]
        return split_const(np.concatenate([np.cos(angle), -np.sin(angle)], axis=0), wide)

    def inverse(first, last):
        angle = np.arange(first, last)[:, None] * theta[None, :]
        return split_const(np.concatenate([np.cos(angle), -np.sin(angle)], axis=1) * (2.0 / size))

    return (
        forward(0, taps),
        forward(taps, size),
        forward(0, rows),
        forward(rows, size, False),
        inverse(taps, size),
        inverse(0, rows),
        inverse(-taps, 0),
    )


def mm(a, b):
    return jnp.dot(a, b, preferred_element_type=F32)


def dft_wide(matrix, x):
    hi = x.astype(BF16)
    lo = (x - hi.astype(F32)).astype(BF16)
    return mm(matrix[...], jnp.concatenate([hi, hi, lo], axis=0))


def dft_half(matrix, x):
    return mm(matrix[:, :2 * x.shape[0]], jnp.concatenate([x, x], axis=0))


def times(a, b):
    half = a.shape[0] // 2
    ar, ai, br, bi = a[:half], a[half:], b[:half], b[half:]
    return jnp.concatenate([ar * br - ai * bi, ar * bi + ai * br], axis=0)


def conj_times(a, b):
    half = a.shape[0] // 2
    ar, ai, br, bi = a[:half], a[half:], b[:half], b[half:]
    return jnp.concatenate([ar * br + ai * bi, ar * bi - ai * br], axis=0)


def low_bit(r):
    return (r & -r).bit_length() - 1


def kernel(
    n_seq, n_tile, n_own, scale,
    xq, xk, xv, cot, weight, sf_in, mf_in, fw_taps_in, fw_tail_in, fw_head_in, fw_after_in, inv_tail_in,
    inv_head_in, inv_taps_in,
    out_ref, gq_ref, gk_ref, gv_ref, gs_ref, gm_ref,
    sf, mf, fw_taps, fw_tail, fw_head, fw_after, inv_tail, inv_head, inv_taps,
    xe, wv, cotv, hspec, gspec, vspec, ks, vs, qs, gated, gg, gmix, ge, gout, part,
    ghalo_s, ghalo_r, mhalo_s, mhalo_r, psend, precv, msend, mrecv, mall, ssend, srecv, sall,
    t_sem, x_sem, w_sem, c_sem, xh_ss, xh_rs, ca_ss, ca_rs, gh_ss, gh_rs, mh_ss, mh_rs,
    eh_ss, eh_rs, p_ss, p_rs, m_ss, m_rs, ma_ss, ma_rs, s_ss, s_rs, sa_ss, sa_rs,
):
    rows, width = ks.shape
    taps = mf.shape[0]
    short = sf.shape[1]
    block = cotv.shape[2]
    bits = n_tile.bit_length() - 1
    x_refs = (xq, xk, xv)
    me = lax.axis_index("seq")
    tile = lax.axis_index("tile")

    def flip(k):
        return tile + (1 << k) - (2 << k) * ((tile // (1 << k)) % 2)

    def relative(r):
        index = tile * 0
        for k in range(bits):
            bit = (tile // (1 << k)) % 2
            index = index + (1 << k) * ((1 - bit) if (r >> k) & 1 else bit)
        return index

    def to_seq(src, dst, send, recv, index):
        return pltpu.make_async_remote_copy(src, dst, send, recv, device_id={"seq": index}, device_id_type=MESH)

    def to_tile(src, dst, send, recv, k):
        return pltpu.make_async_remote_copy(src, dst, send, recv, device_id={"tile": flip(k)}, device_id_type=MESH)

    def lanes(c, size):
        return pl.ds(pl.multiple_of(c * size, size), size)

    def over(size, body):
        def step(c, carry):
            body(c, lanes(c, size))
            return carry
        lax.fori_loop(0, width // size, step, 0)

    table_pairs = (
        (mf_in, mf), (fw_taps_in, fw_taps), (sf_in, sf), (fw_tail_in, fw_tail), (fw_head_in, fw_head),
        (fw_after_in, fw_after), (inv_tail_in, inv_tail), (inv_head_in, inv_head), (inv_taps_in, inv_taps),
    )
    tables = [pltpu.make_async_copy(pair[0], pair[1], t_sem.at[i]) for i, pair in enumerate(table_pairs)]
    for copy in tables[:3]:
        copy.start()
    x_copies = [pltpu.make_async_copy(x_refs[i], xe.at[i, pl.ds(EDGE, rows)], x_sem.at[i]) for i in range(3)]
    for copy in x_copies:
        copy.start()
    own_cot = pltpu.make_async_copy(cot, cotv.at[0], c_sem)
    own_cot.start()
    for copy in tables[3:]:
        copy.start()
    w_copies = []
    for r in range(n_tile):
        columns = pl.ds(pl.multiple_of(relative(r) * block, block), block)
        w_copies.append(pltpu.make_async_copy(weight.at[:, columns], wv.at[r], w_sem.at[r]))
        w_copies[-1].start()

    barrier = pltpu.get_barrier_semaphore()

    def greet(d, carry):
        pl.semaphore_signal(barrier, inc=1, device_id={"seq": (me + d) % n_seq}, device_id_type=MESH)
        return carry
    lax.fori_loop(1, n_seq, greet, 0)
    for k in range(bits):
        pl.semaphore_signal(barrier, inc=1, device_id={"tile": flip(k)}, device_id_type=MESH)
    pl.semaphore_wait(barrier, n_seq - 1 + bits)

    has_next = me < n_seq - 1
    has_prev = me > 0
    nxt = (me + 1) % n_seq
    prv = (me + n_seq - 1) % n_seq

    x_halo = [
        to_seq(x_refs[i].at[pl.ds(rows - EDGE, EDGE)], xe.at[i, pl.ds(0, EDGE)], xh_ss.at[i], xh_rs.at[i], nxt)
        for i in range(3)
    ]

    @pl.when(has_next)
    def _():
        for i in (1, 2, 0):
            x_halo[i].start()

    gather = {}
    for k in reversed(range(bits)):
        gather[1 << k] = to_tile(cot, cotv.at[1 << k], ca_ss.at[1 << k], ca_rs.at[1 << k], k)
        gather[1 << k].start()

    @pl.when(jnp.logical_not(has_prev))
    def _():
        for i in range(3):
            xe[i, pl.ds(0, EDGE), :] = jnp.zeros((EDGE, width), F32)
        ghalo_r[...] = jnp.zeros_like(ghalo_r)

    @pl.when(jnp.logical_not(has_next))
    def _():
        for i in range(3):
            ge[i, pl.ds(rows, EDGE), :] = jnp.zeros((EDGE, width), F32)
        mhalo_r[...] = jnp.zeros_like(mhalo_r)

    for copy in tables[:3]:
        copy.wait()

    def filter_spectrum(c, ls):
        hspec[:, ls] = dft_wide(fw_taps, mf[:, ls])
    over(WIDE, filter_spectrum)

    for copy in x_copies:
        copy.wait()

    @pl.when(has_prev)
    def _():
        for i in range(3):
            x_halo[i].wait_recv()

    def short_conv(i, ls):
        total = sf[i, pl.ds(0, 1), ls] * xe[i, pl.ds(EDGE, rows), ls]
        for j in range(1, short):
            total = total + sf[i, pl.ds(j, 1), ls] * xe[i, pl.ds(EDGE - j, rows), ls]
        return total

    def key_value(c, ls):
        k_rows = short_conv(1, ls)
        ks[:, ls] = k_rows
        v_rows = short_conv(2, ls)
        vs[:, ls] = v_rows
        product = k_rows * v_rows
        gated[:, ls] = product
        ghalo_s[:, ls] = product[rows - taps:].astype(BF16)
    over(LANES, key_value)

    ghalo = to_seq(ghalo_s, ghalo_r, gh_ss, gh_rs, nxt)

    @pl.when(has_next)
    def _():
        ghalo.start()

    def query(c, ls):
        qs[:, ls] = short_conv(0, ls)
    over(LANES, query)

    for copy in tables[3:]:
        copy.wait()

    def gated_spectrum(c, ls):
        gspec[:, ls] = dft_wide(fw_tail, gated[:, ls])
    over(WIDE, gated_spectrum)

    for r in range(n_tile):
        if r == 0:
            own_cot.wait()
        else:
            gather[r].wait_recv()
            for k in reversed(range(low_bit(r))):
                slot = r + (1 << k)
                gather[slot] = to_tile(cotv.at[r], cotv.at[slot], ca_ss.at[slot], ca_rs.at[slot], k)
                gather[slot].start()
        w_copies[r].wait()

        def grad_block(c, ls, r=r):
            term = lax.dot_general(
                cotv[r], wv[r, ls, :], (((1,), (1,)), ((), ())), preferred_element_type=F32
            )
            if r > 0:
                term = term + gg[:, ls]
            gg[:, ls] = term
            if r == n_tile - 1:
                grad_mixed = term * qs[:, ls]
                gmix[:, ls] = grad_mixed
                mhalo_s[:, ls] = grad_mixed[:taps].astype(BF16)
        over(WIDE, grad_block)

    mhalo = to_seq(mhalo_s, mhalo_r, mh_ss, mh_rs, prv)

    @pl.when(has_prev)
    def _():
        mhalo.start()

    @pl.when(has_prev)
    def _():
        ghalo.wait_recv()

    def mixed_rows(c, ls):
        spectrum = gspec[:, ls] + dft_half(fw_taps, ghalo_r[:, ls])
        gspec[:, ls] = spectrum
        mixed = dft_wide(inv_tail, times(spectrum, hspec[:, ls]))
        gout[:, ls] = (qs[:, ls] * mixed).astype(BF16)
        ge[0, pl.ds(0, rows), ls] = gg[:, ls] * mixed
    over(WIDE, mixed_rows)

    e_halo = [
        to_seq(ge.at[i, pl.ds(0, EDGE)], ge.at[i, pl.ds(rows, EDGE)], eh_ss.at[i], eh_rs.at[i], prv) for i in range(3)
    ]

    @pl.when(has_prev)
    def _():
        e_halo[0].start()

    scatter = {}

    def project(r):
        def body(c, carry):
            ds = lanes(c, WIDE)
            term = mm(gout[...], wv[r, :, ds])
            if r & 1:
                psend[r, :, ds] = term.astype(BF16)
            else:
                part[r, :, ds] = term
            return carry
        lax.fori_loop(0, block // WIDE, body, 0)

    def send_sum(r):
        k = low_bit(r)
        scatter[r] = to_tile(psend.at[r], precv.at[r], p_ss.at[r], p_rs.at[r], k)
        scatter[r].start()

    per_wide = WIDE // LANES

    def medium_grad(c, ls):
        v_spec = dft_wide(fw_head, gmix[:, ls])
        vspec[:, ls] = v_spec
        terms = dft_wide(inv_taps, conj_times(gspec[:, ls], v_spec)) * scale
        for p in range(per_wide):
            msend[c * per_wide + p] = terms[:, p * LANES:(p + 1) * LANES].astype(BF16)
    over(WIDE, medium_grad)

    def owner_copy(send, recv, ss, rs, d):
        return to_seq(send.at[(me + d) % n_seq], recv.at[d], ss.at[d], rs.at[d], (me + d) % n_seq)

    def if_owner(index, body):
        if n_own == n_seq:
            body()
        else:
            pl.when(index < n_own)(body)

    def peers(body):
        def step(d, carry):
            body(d)
            return carry
        lax.fori_loop(1, n_seq, step, 0)

    def to_owners(send, recv, ss, rs):
        peers(lambda d: if_owner((me + d) % n_seq, lambda: owner_copy(send, recv, ss, rs, d).start()))

    def from_owner_copy(full, ss, rs, d):
        return to_seq(full.at[me], full.at[me], ss.at[d], rs.at[d], (me + d) % n_seq)

    def owner_sum(send, recv, ss, rs, full, f_ss, f_rs):
        def body():
            def add(d, total):
                owner_copy(send, recv, ss, rs, d).wait_recv()
                return total + recv[d].astype(F32)
            total = lax.fori_loop(1, n_seq, add, send[me].astype(F32))
            full[me] = total.astype(full.dtype)
            peers(lambda d: from_owner_copy(full, f_ss, f_rs, d).start())
        if_owner(me, body)

    def from_owners(full, ss, rs):
        def wait(d):
            source = (me + n_seq - d) % n_seq
            if_owner(source, lambda: to_seq(full.at[source], full.at[source], ss.at[d], rs.at[d], source).wait_recv())
        peers(wait)

    def end_sends(send, recv, ss, rs, full, f_ss, f_rs):
        peers(lambda d: if_owner((me + d) % n_seq, lambda: owner_copy(send, recv, ss, rs, d).wait_send()))
        if_owner(me, lambda: peers(lambda d: from_owner_copy(full, f_ss, f_rs, d).wait_send()))

    medium_set = (msend, mrecv, m_ss, m_rs, mall, ma_ss, ma_rs)
    short_set = (ssend, srecv, s_ss, s_rs, sall, sa_ss, sa_rs)
    to_owners(*medium_set[:4])

    def add_sums(r, first, last):
        total = part[r]
        for k in range(first, last):
            scatter[r + (1 << k)].wait_recv()
            total = total + precv[r + (1 << k)].astype(F32)
        return total

    def step_sums(k):
        for r in range(1 << k, n_tile, 2 << k):
            psend[r] = add_sums(r, 0, k).astype(BF16)
            send_sum(r)

    for r in range(n_tile - 1, 0, -2):
        project(r)
        send_sum(r)

    @pl.when(has_next)
    def _():
        mhalo.wait_recv()

    def product_rows(c, ls):
        spectrum = vspec[:, ls] + dft_half(fw_after, mhalo_r[:, ls])
        grad_prod = dft_wide(inv_head, conj_times(hspec[:, ls], spectrum))
        ge[1, pl.ds(0, rows), ls] = grad_prod * vs[:, ls]
        ge[2, pl.ds(0, rows), ls] = grad_prod * ks[:, ls]
    over(WIDE, product_rows)

    @pl.when(has_prev)
    def _():
        e_halo[1].start()
        e_halo[2].start()

    for r in range(2, n_tile, 2):
        project(r)
    for k in range(1, bits):
        step_sums(k)
    project(0)
    owner_sum(*medium_set)

    def short_grad(c, ls):
        for i in range(3):
            g_rows = ge[i, pl.ds(0, rows), ls] * scale
            for j in range(short):
                ssend[c, pl.ds(i * EDGE + j, 1), :] = jnp.sum(
                    g_rows * xe[i, pl.ds(EDGE - j, rows), ls], axis=0, keepdims=True
                )
            for j in range(short, EDGE):
                ssend[c, pl.ds(i * EDGE + j, 1), :] = jnp.zeros((1, LANES), F32)
    over(LANES, short_grad)
    to_owners(*short_set[:4])

    @pl.when(has_next)
    def _():
        for i in range(3):
            e_halo[i].wait_recv()

    outs = (gq_ref, gk_ref, gv_ref)

    def feature_grad(c, ls):
        for i in range(3):
            total = sf[i, pl.ds(0, 1), ls] * ge[i, pl.ds(0, rows), ls]
            for j in range(1, short):
                total = total + sf[i, pl.ds(j, 1), ls] * ge[i, pl.ds(j, rows), ls]
            outs[i][:, ls] = total
    over(LANES, feature_grad)

    owner_sum(*short_set)
    out_ref[...] = add_sums(0, 0, bits)

    from_owners(mall, ma_ss, ma_rs)
    from_owners(sall, sa_ss, sa_rs)

    for o in range(n_own):
        columns = slice(o * LANES, (o + 1) * LANES)
        gm_ref[:, columns] = mall[o].astype(F32)
        for i in range(3):
            gs_ref[i, :, columns] = sall[o, i * EDGE:i * EDGE + short]

    end_sends(*medium_set)
    end_sends(*short_set)
    for r in range(1, n_tile):
        gather[r].wait_send()
        scatter[r].wait_send()

    @pl.when(has_next)
    def _():
        for i in range(3):
            x_halo[i].wait_send()
        ghalo.wait_send()

    @pl.when(has_prev)
    def _():
        for i in range(3):
            e_halo[i].wait_send()
        mhalo.wait_send()


def write_results(*refs):
    count = len(refs) // 2
    sems = refs[-1]
    copies = [pltpu.make_async_copy(refs[i], refs[count + i], sems.at[i]) for i in range(count)]
    for copy in copies:
        copy.start()
    for copy in copies:
        copy.wait()


def shards(n_seq, n_tile, query_feat, key_feat, value_feat, short_filter, medium_filter, out_weight, cotangent):
    rows, width = query_feat.shape
    short = short_filter.shape[1]
    taps = medium_filter.shape[0]
    block = cotangent.shape[1]
    size = rows + taps
    n_own = width // LANES
    assert n_own <= n_seq and short <= EDGE and rows >= taps
    scale = 1.0 / math.sqrt(n_seq * rows)
    consts = dft_consts(rows, taps)
    hbm = pl.BlockSpec(memory_space=pltpu.HBM)
    vmem = pl.BlockSpec(memory_space=pltpu.VMEM)
    dma = pltpu.SemaphoreType.DMA
    results = pl.pallas_call(
        functools.partial(kernel, n_seq, n_tile, n_own, scale),
        out_shape=(
            pltpu.VMEM((rows, block), F32),
            pltpu.VMEM((rows, width), F32),
            pltpu.VMEM((rows, width), F32),
            pltpu.VMEM((rows, width), F32),
            pltpu.VMEM(short_filter.shape, F32),
            pltpu.VMEM(medium_filter.shape, F32),
        ),
        in_specs=[hbm] * 14,
        out_specs=[vmem] * 6,
        scratch_shapes=[
            pltpu.VMEM(short_filter.shape, F32),
            pltpu.VMEM(medium_filter.shape, F32),
            *[pltpu.VMEM(c.shape, BF16) for c in consts],
            pltpu.VMEM((3, rows + EDGE, width), F32),
            pltpu.VMEM((n_tile, width, block), BF16),
            pltpu.VMEM((n_tile, rows, block), BF16),
            pltpu.VMEM((size, width), F32),
            pltpu.VMEM((size, width), F32),
            pltpu.VMEM((size, width), F32),
            pltpu.VMEM((rows, width), F32),
            pltpu.VMEM((rows, width), F32),
            pltpu.VMEM((rows, width), F32),
            pltpu.VMEM((rows, width), F32),
            pltpu.VMEM((rows, width), F32),
            pltpu.VMEM((rows, width), F32),
            pltpu.VMEM((3, rows + EDGE, width), F32),
            pltpu.VMEM((rows, width), BF16),
            pltpu.VMEM((n_tile, rows, block), F32),
            pltpu.VMEM((taps, width), BF16),
            pltpu.VMEM((taps, width), BF16),
            pltpu.VMEM((taps, width), BF16),
            pltpu.VMEM((taps, width), BF16),
            pltpu.VMEM((n_tile, rows, block), BF16),
            pltpu.VMEM((n_tile, rows, block), BF16),
            pltpu.VMEM((n_own, taps, LANES), BF16),
            pltpu.VMEM((n_seq, taps, LANES), BF16),
            pltpu.VMEM((n_own, taps, LANES), BF16),
            pltpu.VMEM((n_own, 3 * EDGE, LANES), F32),
            pltpu.VMEM((n_seq, 3 * EDGE, LANES), F32),
            pltpu.VMEM((n_own, 3 * EDGE, LANES), F32),
            dma((9,)),
            dma((3,)),
            dma((n_tile,)),
            dma,
            dma((3,)),
            dma((3,)),
            dma((n_tile,)),
            dma((n_tile,)),
            dma,
            dma,
            dma,
            dma,
            dma((3,)),
            dma((3,)),
            dma((n_tile,)),
            dma((n_tile,)),
            *[dma((n_seq,)) for _ in range(8)],
        ],
        compiler_params=pltpu.CompilerParams(
            collective_id=0, has_side_effects=True, vmem_limit_bytes=60 * 1024 * 1024
        ),
    )(
        query_feat, key_feat, value_feat, cotangent, out_weight, short_filter, medium_filter,
        *[jnp.asarray(c) for c in consts],
    )
    return pl.pallas_call(
        write_results,
        out_shape=tuple(jax.ShapeDtypeStruct(r.shape, r.dtype) for r in results),
        in_specs=[pl.BlockSpec(memory_space=pl.ANY)] * len(results),
        out_specs=[hbm] * len(results),
        scratch_shapes=[dma((len(results),))],
        compiler_params=pltpu.CompilerParams(vmem_limit_bytes=8 * 1024 * 1024),
    )(*results)


def solution(mesh):
    in_specs = (
        P("seq", "tile"),
        P("seq", "tile"),
        P("seq", "tile"),
        P(None, None, "tile"),
        P(None, "tile"),
        P("tile", None),
        P("seq", "tile"),
    )
    out_specs = (
        P("seq", "tile"),
        P("seq", "tile"),
        P("seq", "tile"),
        P("seq", "tile"),
        P(None, None, "tile"),
        P(None, "tile"),
    )
    body = functools.partial(shards, mesh.shape["seq"], mesh.shape["tile"])
    return jax.shard_map(body, mesh=mesh, in_specs=in_specs, out_specs=out_specs, check_vma=False)
```

```python
import functools
import math

import jax
import jax.numpy as jnp
import ml_dtypes
import numpy as np
from jax import lax
from jax.experimental import pallas as pl
from jax.experimental.pallas import tpu as pltpu
from jax.sharding import PartitionSpec as P

MESH = pl.DeviceIdType.MESH
F32 = jnp.float32
BF16 = jnp.bfloat16
LANES = 128
WIDE = 512
EDGE = 8


def split_const(matrix, wide=True):
    hi = matrix.astype(np.float32).astype(ml_dtypes.bfloat16)
    lo = (matrix - hi.astype(np.float64)).astype(np.float32).astype(ml_dtypes.bfloat16)
    return np.concatenate([hi, lo, hi] if wide else [hi, lo], axis=1)


def dft_consts(rows, taps):
    size = rows + taps
    theta = 2.0 * np.pi * (np.arange(size // 2) + 0.5) / size

    def forward(first, last, wide=True):
        angle = theta[:, None] * np.arange(first, last)[None, :]
        return split_const(np.concatenate([np.cos(angle), -np.sin(angle)], axis=0), wide)

    def inverse(first, last):
        angle = np.arange(first, last)[:, None] * theta[None, :]
        return split_const(np.concatenate([np.cos(angle), -np.sin(angle)], axis=1) * (2.0 / size))

    return (
        forward(0, taps),
        forward(taps, size),
        forward(0, rows),
        forward(rows, size, False),
        inverse(taps, size),
        inverse(0, rows),
        inverse(-taps, 0),
    )


def mm(a, b):
    return jnp.dot(a, b, preferred_element_type=F32)


def dft_wide(matrix, x):
    hi = x.astype(BF16)
    lo = (x - hi.astype(F32)).astype(BF16)
    return mm(matrix[...], jnp.concatenate([hi, hi, lo], axis=0))


def dft_half(matrix, x):
    return mm(matrix[:, :2 * x.shape[0]], jnp.concatenate([x, x], axis=0))


def times(a, b):
    half = a.shape[0] // 2
    ar, ai, br, bi = a[:half], a[half:], b[:half], b[half:]
    return jnp.concatenate([ar * br - ai * bi, ar * bi + ai * br], axis=0)


def conj_times(a, b):
    half = a.shape[0] // 2
    ar, ai, br, bi = a[:half], a[half:], b[:half], b[half:]
    return jnp.concatenate([ar * br + ai * bi, ar * bi - ai * br], axis=0)


def low_bit(r):
    return (r & -r).bit_length() - 1


def kernel(
    n_seq, n_tile, n_own, scale,
    xq, xk, xv, cot, weight, sf_in, mf_in, fw_taps_in, fw_tail_in, fw_head_in, fw_after_in, inv_tail_in,
    inv_head_in, inv_taps_in,
    out_ref, gq_ref, gk_ref, gv_ref, gs_ref, gm_ref,
    sf, mf, fw_taps, fw_tail, fw_head, fw_after, inv_tail, inv_head, inv_taps,
    xe, wv, cotv, hspec, gspec, vspec, ks, vs, qs, gated, gg, gmix, ge, gout, part,
    ghalo_s, ghalo_r, mhalo_s, mhalo_r, psend, precv, msend, mrecv, mall, ssend, srecv, sall,
    t_sem, x_sem, w_sem, c_sem, xh_ss, xh_rs, ca_ss, ca_rs, gh_ss, gh_rs, mh_ss, mh_rs,
    eh_ss, eh_rs, p_ss, p_rs, m_ss, m_rs, ma_ss, ma_rs, s_ss, s_rs, sa_ss, sa_rs,
):
    rows, width = ks.shape
    taps = mf.shape[0]
    short = sf.shape[1]
    block = cotv.shape[2]
    bits = n_tile.bit_length() - 1
    x_refs = (xq, xk, xv)
    me = lax.axis_index("seq")
    tile = lax.axis_index("tile")

    def flip(k):
        return tile + (1 << k) - (2 << k) * ((tile // (1 << k)) % 2)

    def relative(r):
        index = tile * 0
        for k in range(bits):
            bit = (tile // (1 << k)) % 2
            index = index + (1 << k) * ((1 - bit) if (r >> k) & 1 else bit)
        return index

    def to_seq(src, dst, send, recv, index):
        return pltpu.make_async_remote_copy(src, dst, send, recv, device_id={"seq": index}, device_id_type=MESH)

    def to_tile(src, dst, send, recv, k):
        return pltpu.make_async_remote_copy(src, dst, send, recv, device_id={"tile": flip(k)}, device_id_type=MESH)

    def lanes(c, size):
        return pl.ds(pl.multiple_of(c * size, size), size)

    def over(size, body):
        def step(c, carry):
            body(c, lanes(c, size))
            return carry
        lax.fori_loop(0, width // size, step, 0)

    def parts(c):
        return [pl.ds(pl.multiple_of(c * WIDE + p * LANES, LANES), LANES) for p in range(WIDE // LANES)]

    table_pairs = (
        (mf_in, mf), (fw_taps_in, fw_taps), (sf_in, sf), (fw_tail_in, fw_tail), (fw_head_in, fw_head),
        (fw_after_in, fw_after), (inv_tail_in, inv_tail), (inv_head_in, inv_head), (inv_taps_in, inv_taps),
    )
    tables = [pltpu.make_async_copy(pair[0], pair[1], t_sem.at[i]) for i, pair in enumerate(table_pairs)]
    for copy in tables[:3]:
        copy.start()
    x_copies = [pltpu.make_async_copy(x_refs[i], xe.at[i, pl.ds(EDGE, rows)], x_sem.at[i]) for i in range(3)]
    for copy in x_copies:
        copy.start()
    own_cot = pltpu.make_async_copy(cot, cotv.at[0], c_sem)
    own_cot.start()
    for copy in tables[3:]:
        copy.start()
    w_copies = []
    for r in range(n_tile):
        columns = pl.ds(pl.multiple_of(relative(r) * block, block), block)
        w_copies.append(pltpu.make_async_copy(weight.at[:, columns], wv.at[r], w_sem.at[r]))
        w_copies[-1].start()

    barrier = pltpu.get_barrier_semaphore()

    def greet(d, carry):
        pl.semaphore_signal(barrier, inc=1, device_id={"seq": (me + d) % n_seq}, device_id_type=MESH)
        return carry
    lax.fori_loop(1, n_seq, greet, 0)
    for k in range(bits):
        pl.semaphore_signal(barrier, inc=1, device_id={"tile": flip(k)}, device_id_type=MESH)
    pl.semaphore_wait(barrier, n_seq - 1 + bits)

    has_next = me < n_seq - 1
    has_prev = me > 0
    nxt = (me + 1) % n_seq
    prv = (me + n_seq - 1) % n_seq

    x_halo = [
        to_seq(x_refs[i].at[pl.ds(rows - EDGE, EDGE)], xe.at[i, pl.ds(0, EDGE)], xh_ss.at[i], xh_rs.at[i], nxt)
        for i in range(3)
    ]

    @pl.when(has_next)
    def _():
        for i in (1, 2, 0):
            x_halo[i].start()

    gather = {}
    for k in reversed(range(bits)):
        gather[1 << k] = to_tile(cot, cotv.at[1 << k], ca_ss.at[1 << k], ca_rs.at[1 << k], k)
        gather[1 << k].start()

    @pl.when(jnp.logical_not(has_prev))
    def _():
        for i in range(3):
            xe[i, pl.ds(0, EDGE), :] = jnp.zeros((EDGE, width), F32)
        ghalo_r[...] = jnp.zeros_like(ghalo_r)

    @pl.when(jnp.logical_not(has_next))
    def _():
        for i in range(3):
            ge[i, pl.ds(rows, EDGE), :] = jnp.zeros((EDGE, width), F32)
        mhalo_r[...] = jnp.zeros_like(mhalo_r)

    for copy in tables[:3]:
        copy.wait()

    for copy in x_copies:
        copy.wait()

    @pl.when(has_prev)
    def _():
        for i in range(3):
            x_halo[i].wait_recv()

    def short_conv(i, ls):
        total = sf[i, pl.ds(0, 1), ls] * xe[i, pl.ds(EDGE, rows), ls]
        for j in range(1, short):
            total = total + sf[i, pl.ds(j, 1), ls] * xe[i, pl.ds(EDGE - j, rows), ls]
        return total

    def key_value(c, ls):
        hspec[:, ls] = dft_wide(fw_taps, mf[:, ls])
        for sub in parts(c):
            k_rows = short_conv(1, sub)
            ks[:, sub] = k_rows
            v_rows = short_conv(2, sub)
            vs[:, sub] = v_rows
            product = k_rows * v_rows
            gated[:, sub] = product
            ghalo_s[:, sub] = product[rows - taps:].astype(BF16)
    over(WIDE, key_value)

    ghalo = to_seq(ghalo_s, ghalo_r, gh_ss, gh_rs, nxt)

    @pl.when(has_next)
    def _():
        ghalo.start()

    for copy in tables[3:]:
        copy.wait()

    for r in range(n_tile):
        if r == 0:
            own_cot.wait()
        else:
            gather[r].wait_recv()
            for k in reversed(range(low_bit(r))):
                slot = r + (1 << k)
                gather[slot] = to_tile(cotv.at[r], cotv.at[slot], ca_ss.at[slot], ca_rs.at[slot], k)
                gather[slot].start()
        w_copies[r].wait()

        def grad_block(c, ls, r=r):
            term = lax.dot_general(
                cotv[r], wv[r, ls, :], (((1,), (1,)), ((), ())), preferred_element_type=F32
            )
            if r > 0:
                term = term + gg[:, ls]
            else:
                gspec[:, ls] = dft_wide(fw_tail, gated[:, ls])
                for sub in parts(c):
                    qs[:, sub] = short_conv(0, sub)
            gg[:, ls] = term
            if r == n_tile - 1:
                grad_mixed = term * qs[:, ls]
                gmix[:, ls] = grad_mixed
                mhalo_s[:, ls] = grad_mixed[:taps].astype(BF16)
        over(WIDE, grad_block)

    mhalo = to_seq(mhalo_s, mhalo_r, mh_ss, mh_rs, prv)

    @pl.when(has_prev)
    def _():
        mhalo.start()

    @pl.when(has_prev)
    def _():
        ghalo.wait_recv()

    per_wide = WIDE // LANES

    def mixed_rows(c, ls):
        v_spec = dft_wide(fw_head, gmix[:, ls])
        vspec[:, ls] = v_spec
        spectrum = gspec[:, ls] + dft_half(fw_taps, ghalo_r[:, ls])
        mixed = dft_wide(inv_tail, times(spectrum, hspec[:, ls]))
        gout[:, ls] = (qs[:, ls] * mixed).astype(BF16)
        ge[0, pl.ds(0, rows), ls] = gg[:, ls] * mixed
        terms = (dft_wide(inv_taps, conj_times(spectrum, v_spec)) * scale).astype(BF16)
        for p in range(per_wide):
            msend[c * per_wide + p] = terms[:, p * LANES:(p + 1) * LANES]
    over(WIDE, mixed_rows)

    e_halo = [
        to_seq(ge.at[i, pl.ds(0, EDGE)], ge.at[i, pl.ds(rows, EDGE)], eh_ss.at[i], eh_rs.at[i], prv) for i in range(3)
    ]

    @pl.when(has_prev)
    def _():
        e_halo[0].start()

    scatter = {}

    def project(r, beside=None):
        def body(c, carry):
            ds = lanes(c, WIDE)
            if beside is not None:
                beside(c, ds)
            term = mm(gout[...], wv[r, :, ds])
            if r & 1:
                psend[r, :, ds] = term.astype(BF16)
            else:
                part[r, :, ds] = term
            return carry
        lax.fori_loop(0, block // WIDE, body, 0)

    def send_sum(r):
        k = low_bit(r)
        scatter[r] = to_tile(psend.at[r], precv.at[r], p_ss.at[r], p_rs.at[r], k)
        scatter[r].start()

    def owner_copy(send, recv, ss, rs, d):
        return to_seq(send.at[(me + d) % n_seq], recv.at[d], ss.at[d], rs.at[d], (me + d) % n_seq)

    def if_owner(index, body):
        if n_own == n_seq:
            body()
        else:
            pl.when(index < n_own)(body)

    def peers(body):
        def step(d, carry):
            body(d)
            return carry
        lax.fori_loop(1, n_seq, step, 0)

    def to_owners(send, recv, ss, rs):
        peers(lambda d: if_owner((me + d) % n_seq, lambda: owner_copy(send, recv, ss, rs, d).start()))

    def from_owner_copy(full, ss, rs, d):
        return to_seq(full.at[me], full.at[me], ss.at[d], rs.at[d], (me + d) % n_seq)

    def owner_sum(send, recv, ss, rs, full, f_ss, f_rs):
        def body():
            def add(d, total):
                owner_copy(send, recv, ss, rs, d).wait_recv()
                return total + recv[d].astype(F32)
            total = lax.fori_loop(1, n_seq, add, send[me].astype(F32))
            full[me] = total.astype(full.dtype)
            peers(lambda d: from_owner_copy(full, f_ss, f_rs, d).start())
        if_owner(me, body)

    def from_owners(full, ss, rs):
        def wait(d):
            source = (me + n_seq - d) % n_seq
            if_owner(source, lambda: to_seq(full.at[source], full.at[source], ss.at[d], rs.at[d], source).wait_recv())
        peers(wait)

    def end_sends(send, recv, ss, rs, full, f_ss, f_rs):
        peers(lambda d: if_owner((me + d) % n_seq, lambda: owner_copy(send, recv, ss, rs, d).wait_send()))
        if_owner(me, lambda: peers(lambda d: from_owner_copy(full, f_ss, f_rs, d).wait_send()))

    medium_set = (msend, mrecv, m_ss, m_rs, mall, ma_ss, ma_rs)
    short_set = (ssend, srecv, s_ss, s_rs, sall, sa_ss, sa_rs)
    to_owners(*medium_set[:4])

    def add_sums(r, first, last):
        total = part[r]
        for k in range(first, last):
            scatter[r + (1 << k)].wait_recv()
            total = total + precv[r + (1 << k)].astype(F32)
        return total

    def step_sums(k):
        for r in range(1 << k, n_tile, 2 << k):
            psend[r] = add_sums(r, 0, k).astype(BF16)
            send_sum(r)

    def short_grad(i, c):
        for p, sub in enumerate(parts(c)):
            g_rows = ge[i, pl.ds(0, rows), sub] * scale
            for j in range(short):
                ssend[c * per_wide + p, pl.ds(i * EDGE + j, 1), :] = jnp.sum(
                    g_rows * xe[i, pl.ds(EDGE - j, rows), sub], axis=0, keepdims=True
                )
            for j in range(short, EDGE):
                ssend[c * per_wide + p, pl.ds(i * EDGE + j, 1), :] = jnp.zeros((1, LANES), F32)

    outs = (gq_ref, gk_ref, gv_ref)

    def feature_grad(i, c):
        for sub in parts(c):
            total = sf[i, pl.ds(0, 1), sub] * ge[i, pl.ds(0, rows), sub]
            for j in range(1, short):
                total = total + sf[i, pl.ds(j, 1), sub] * ge[i, pl.ds(j, rows), sub]
            outs[i][:, sub] = total

    for r in range(n_tile - 1, 0, -2):
        project(r, (lambda c, ls: short_grad(0, c)) if r == n_tile - 1 else None)
        send_sum(r)

    @pl.when(has_next)
    def _():
        mhalo.wait_recv()
        e_halo[0].wait_recv()

    def product_rows(c, ls):
        spectrum = vspec[:, ls] + dft_half(fw_after, mhalo_r[:, ls])
        grad_prod = dft_wide(inv_head, conj_times(hspec[:, ls], spectrum))
        ge[1, pl.ds(0, rows), ls] = grad_prod * vs[:, ls]
        ge[2, pl.ds(0, rows), ls] = grad_prod * ks[:, ls]
        feature_grad(0, c)

    project(2 % n_tile, product_rows)

    @pl.when(has_prev)
    def _():
        e_halo[1].start()
        e_halo[2].start()

    for r in range(4, n_tile, 2):
        project(r)
    for k in range(1, bits):
        step_sums(k)
    owner_sum(*medium_set)

    def last_short(c, ls):
        short_grad(1, c)
        short_grad(2, c)

    project(0, last_short)
    to_owners(*short_set[:4])

    @pl.when(has_next)
    def _():
        e_halo[1].wait_recv()
        e_halo[2].wait_recv()

    def last_features(c, ls):
        feature_grad(1, c)
        feature_grad(2, c)
    over(WIDE, last_features)

    owner_sum(*short_set)
    out_ref[...] = add_sums(0, 0, bits)

    from_owners(mall, ma_ss, ma_rs)
    from_owners(sall, sa_ss, sa_rs)

    for o in range(n_own):
        columns = slice(o * LANES, (o + 1) * LANES)
        gm_ref[:, columns] = mall[o].astype(F32)
        for i in range(3):
            gs_ref[i, :, columns] = sall[o, i * EDGE:i * EDGE + short]

    end_sends(*medium_set)
    end_sends(*short_set)
    for r in range(1, n_tile):
        gather[r].wait_send()
        scatter[r].wait_send()

    @pl.when(has_next)
    def _():
        for i in range(3):
            x_halo[i].wait_send()
        ghalo.wait_send()

    @pl.when(has_prev)
    def _():
        for i in range(3):
            e_halo[i].wait_send()
        mhalo.wait_send()


def write_results(*refs):
    count = len(refs) // 2
    sems = refs[-1]
    copies = [pltpu.make_async_copy(refs[i], refs[count + i], sems.at[i]) for i in range(count)]
    for copy in copies:
        copy.start()
    for copy in copies:
        copy.wait()


def shards(n_seq, n_tile, query_feat, key_feat, value_feat, short_filter, medium_filter, out_weight, cotangent):
    rows, width = query_feat.shape
    short = short_filter.shape[1]
    taps = medium_filter.shape[0]
    block = cotangent.shape[1]
    size = rows + taps
    n_own = width // LANES
    assert width == block and n_tile >= 4
    assert n_own <= n_seq and short <= EDGE and rows >= taps
    scale = 1.0 / math.sqrt(n_seq * rows)
    consts = dft_consts(rows, taps)
    hbm = pl.BlockSpec(memory_space=pltpu.HBM)
    vmem = pl.BlockSpec(memory_space=pltpu.VMEM)
    dma = pltpu.SemaphoreType.DMA
    results = pl.pallas_call(
        functools.partial(kernel, n_seq, n_tile, n_own, scale),
        out_shape=(
            pltpu.VMEM((rows, block), F32),
            pltpu.VMEM((rows, width), F32),
            pltpu.VMEM((rows, width), F32),
            pltpu.VMEM((rows, width), F32),
            pltpu.VMEM(short_filter.shape, F32),
            pltpu.VMEM(medium_filter.shape, F32),
        ),
        in_specs=[hbm] * 14,
        out_specs=[vmem] * 6,
        scratch_shapes=[
            pltpu.VMEM(short_filter.shape, F32),
            pltpu.VMEM(medium_filter.shape, F32),
            *[pltpu.VMEM(c.shape, BF16) for c in consts],
            pltpu.VMEM((3, rows + EDGE, width), F32),
            pltpu.VMEM((n_tile, width, block), BF16),
            pltpu.VMEM((n_tile, rows, block), BF16),
            pltpu.VMEM((size, width), F32),
            pltpu.VMEM((size, width), F32),
            pltpu.VMEM((size, width), F32),
            pltpu.VMEM((rows, width), F32),
            pltpu.VMEM((rows, width), F32),
            pltpu.VMEM((rows, width), F32),
            pltpu.VMEM((rows, width), F32),
            pltpu.VMEM((rows, width), F32),
            pltpu.VMEM((rows, width), F32),
            pltpu.VMEM((3, rows + EDGE, width), F32),
            pltpu.VMEM((rows, width), BF16),
            pltpu.VMEM((n_tile, rows, block), F32),
            pltpu.VMEM((taps, width), BF16),
            pltpu.VMEM((taps, width), BF16),
            pltpu.VMEM((taps, width), BF16),
            pltpu.VMEM((taps, width), BF16),
            pltpu.VMEM((n_tile, rows, block), BF16),
            pltpu.VMEM((n_tile, rows, block), BF16),
            pltpu.VMEM((n_own, taps, LANES), BF16),
            pltpu.VMEM((n_seq, taps, LANES), BF16),
            pltpu.VMEM((n_own, taps, LANES), BF16),
            pltpu.VMEM((n_own, 3 * EDGE, LANES), F32),
            pltpu.VMEM((n_seq, 3 * EDGE, LANES), F32),
            pltpu.VMEM((n_own, 3 * EDGE, LANES), F32),
            dma((9,)),
            dma((3,)),
            dma((n_tile,)),
            dma,
            dma((3,)),
            dma((3,)),
            dma((n_tile,)),
            dma((n_tile,)),
            dma,
            dma,
            dma,
            dma,
            dma((3,)),
            dma((3,)),
            dma((n_tile,)),
            dma((n_tile,)),
            *[dma((n_seq,)) for _ in range(8)],
        ],
        compiler_params=pltpu.CompilerParams(
            collective_id=0, has_side_effects=True, vmem_limit_bytes=60 * 1024 * 1024
        ),
    )(
        query_feat, key_feat, value_feat, cotangent, out_weight, short_filter, medium_filter,
        *[jnp.asarray(c) for c in consts],
    )
    return pl.pallas_call(
        write_results,
        out_shape=tuple(jax.ShapeDtypeStruct(r.shape, r.dtype) for r in results),
        in_specs=[pl.BlockSpec(memory_space=pl.ANY)] * len(results),
        out_specs=[hbm] * len(results),
        scratch_shapes=[dma((len(results),))],
        compiler_params=pltpu.CompilerParams(vmem_limit_bytes=8 * 1024 * 1024),
    )(*results)


def solution(mesh):
    in_specs = (
        P("seq", "tile"),
        P("seq", "tile"),
        P("seq", "tile"),
        P(None, None, "tile"),
        P(None, "tile"),
        P("tile", None),
        P("seq", "tile"),
    )
    out_specs = (
        P("seq", "tile"),
        P("seq", "tile"),
        P("seq", "tile"),
        P("seq", "tile"),
        P(None, None, "tile"),
        P(None, "tile"),
    )
    body = functools.partial(shards, mesh.shape["seq"], mesh.shape["tile"])
    return jax.shard_map(body, mesh=mesh, in_specs=in_specs, out_specs=out_specs, check_vma=False)
```

```python
import functools
import math

import jax
import jax.numpy as jnp
import ml_dtypes
import numpy as np
from jax import lax
from jax.experimental import pallas as pl
from jax.experimental.pallas import tpu as pltpu
from jax.sharding import PartitionSpec as P

MESH = pl.DeviceIdType.MESH
F32 = jnp.float32
BF16 = jnp.bfloat16
LANES = 128
WIDE = 512
EDGE = 8


def split_const(matrix, wide=True):
    hi = matrix.astype(np.float32).astype(ml_dtypes.bfloat16)
    lo = (matrix - hi.astype(np.float64)).astype(np.float32).astype(ml_dtypes.bfloat16)
    return np.concatenate([hi, lo, hi] if wide else [hi, lo], axis=1)


def dft_consts(rows, taps):
    size = rows + taps
    theta = 2.0 * np.pi * (np.arange(size // 2) + 0.5) / size

    def forward(first, last, wide=True):
        angle = theta[:, None] * np.arange(first, last)[None, :]
        return split_const(np.concatenate([np.cos(angle), -np.sin(angle)], axis=0), wide)

    def inverse(first, last):
        angle = np.arange(first, last)[:, None] * theta[None, :]
        return split_const(np.concatenate([np.cos(angle), -np.sin(angle)], axis=1) * (2.0 / size))

    return (
        forward(0, taps),
        forward(taps, size),
        forward(0, rows),
        forward(rows, size, False),
        inverse(taps, size),
        inverse(0, rows),
        inverse(-taps, 0),
    )


def mm(a, b):
    return jnp.dot(a, b, preferred_element_type=F32)


def dft_wide(matrix, x):
    hi = x.astype(BF16)
    lo = (x - hi.astype(F32)).astype(BF16)
    return mm(matrix[...], jnp.concatenate([hi, hi, lo], axis=0))


def dft_half(matrix, x):
    return mm(matrix[:, :2 * x.shape[0]], jnp.concatenate([x, x], axis=0))


def times(a, b):
    half = a.shape[0] // 2
    ar, ai, br, bi = a[:half], a[half:], b[:half], b[half:]
    return jnp.concatenate([ar * br - ai * bi, ar * bi + ai * br], axis=0)


def conj_times(a, b):
    half = a.shape[0] // 2
    ar, ai, br, bi = a[:half], a[half:], b[:half], b[half:]
    return jnp.concatenate([ar * br + ai * bi, ar * bi - ai * br], axis=0)


def low_bit(r):
    return (r & -r).bit_length() - 1


def kernel(
    n_seq, n_tile, n_own, scale,
    xq, xk, xv, cot, weight, sf_in, mf_in, fw_taps_in, fw_tail_in, fw_head_in, fw_after_in, inv_tail_in,
    inv_head_in, inv_taps_in,
    out_ref, gq_ref, gk_ref, gv_ref, gs_ref, gm_ref,
    sf, mf, fw_taps, fw_tail, fw_head, fw_after, inv_tail, inv_head, inv_taps,
    xe, wv, cotv, hspec, gspec, vspec, ks, vs, qs, gated, gg, gmix, mix, ge, gout, part,
    ghalo_s, ghalo_r, mhalo_s, mhalo_r, psend, precv, msend, mrecv, mall, ssend, srecv, sall,
    t_sem, x_sem, w_sem, c_sem, xh_ss, xh_rs, ca_ss, ca_rs, gh_ss, gh_rs, mh_ss, mh_rs,
    eh_ss, eh_rs, p_ss, p_rs, m_ss, m_rs, ma_ss, ma_rs, s_ss, s_rs, sa_ss, sa_rs,
):
    rows, width = ks.shape
    taps = mf.shape[0]
    short = sf.shape[1]
    block = cotv.shape[2]
    bits = n_tile.bit_length() - 1
    x_refs = (xq, xk, xv)
    me = lax.axis_index("seq")
    tile = lax.axis_index("tile")

    def flip(k):
        return tile + (1 << k) - (2 << k) * ((tile // (1 << k)) % 2)

    def relative(r):
        index = tile * 0
        for k in range(bits):
            bit = (tile // (1 << k)) % 2
            index = index + (1 << k) * ((1 - bit) if (r >> k) & 1 else bit)
        return index

    def to_seq(src, dst, send, recv, index):
        return pltpu.make_async_remote_copy(src, dst, send, recv, device_id={"seq": index}, device_id_type=MESH)

    def to_tile(src, dst, send, recv, k):
        return pltpu.make_async_remote_copy(src, dst, send, recv, device_id={"tile": flip(k)}, device_id_type=MESH)

    def lanes(c, size):
        return pl.ds(pl.multiple_of(c * size, size), size)

    def over(size, body):
        def step(c, carry):
            body(c, lanes(c, size))
            return carry
        lax.fori_loop(0, width // size, step, 0)

    def parts(c):
        return [pl.ds(pl.multiple_of(c * WIDE + p * LANES, LANES), LANES) for p in range(WIDE // LANES)]

    table_pairs = (
        (mf_in, mf), (fw_taps_in, fw_taps), (sf_in, sf), (fw_tail_in, fw_tail), (fw_head_in, fw_head),
        (fw_after_in, fw_after), (inv_tail_in, inv_tail), (inv_head_in, inv_head), (inv_taps_in, inv_taps),
    )
    tables = [pltpu.make_async_copy(pair[0], pair[1], t_sem.at[i]) for i, pair in enumerate(table_pairs)]
    for copy in tables[:3]:
        copy.start()
    x_copies = [pltpu.make_async_copy(x_refs[i], xe.at[i, pl.ds(EDGE, rows)], x_sem.at[i]) for i in range(3)]
    for copy in x_copies:
        copy.start()
    own_cot = pltpu.make_async_copy(cot, cotv.at[0], c_sem)
    own_cot.start()
    barrier = pltpu.get_barrier_semaphore()

    def greet(d, carry):
        pl.semaphore_signal(barrier, inc=1, device_id={"seq": (me + d) % n_seq}, device_id_type=MESH)
        return carry
    lax.fori_loop(1, n_seq, greet, 0)
    for k in range(bits):
        pl.semaphore_signal(barrier, inc=1, device_id={"tile": flip(k)}, device_id_type=MESH)
    pl.semaphore_wait(barrier, n_seq - 1 + bits)

    has_next = me < n_seq - 1
    has_prev = me > 0
    nxt = (me + 1) % n_seq
    prv = (me + n_seq - 1) % n_seq

    x_halo = [
        to_seq(x_refs[i].at[pl.ds(rows - EDGE, EDGE)], xe.at[i, pl.ds(0, EDGE)], xh_ss.at[i], xh_rs.at[i], nxt)
        for i in range(3)
    ]

    @pl.when(has_next)
    def _():
        for i in (1, 2, 0):
            x_halo[i].start()

    gather = {}
    for k in reversed(range(bits)):
        gather[1 << k] = to_tile(cot, cotv.at[1 << k], ca_ss.at[1 << k], ca_rs.at[1 << k], k)
        gather[1 << k].start()

    for copy in tables[3:]:
        copy.start()
    w_copies = []
    for r in range(n_tile):
        columns = pl.ds(pl.multiple_of(relative(r) * block, block), block)
        w_copies.append(pltpu.make_async_copy(weight.at[:, columns], wv.at[r], w_sem.at[r]))
        w_copies[-1].start()

    @pl.when(jnp.logical_not(has_prev))
    def _():
        for i in range(3):
            xe[i, pl.ds(0, EDGE), :] = jnp.zeros((EDGE, width), F32)
        ghalo_r[...] = jnp.zeros_like(ghalo_r)

    @pl.when(jnp.logical_not(has_next))
    def _():
        for i in range(3):
            ge[i, pl.ds(rows, EDGE), :] = jnp.zeros((EDGE, width), F32)
        mhalo_r[...] = jnp.zeros_like(mhalo_r)

    for copy in tables[:3]:
        copy.wait()

    for copy in x_copies:
        copy.wait()

    @pl.when(has_prev)
    def _():
        for i in range(3):
            x_halo[i].wait_recv()

    def short_conv(i, ls):
        total = sf[i, pl.ds(0, 1), ls] * xe[i, pl.ds(EDGE, rows), ls]
        for j in range(1, short):
            total = total + sf[i, pl.ds(j, 1), ls] * xe[i, pl.ds(EDGE - j, rows), ls]
        return total

    def key_value(c, ls):
        hspec[:, ls] = dft_wide(fw_taps, mf[:, ls])
        for sub in parts(c):
            k_rows = short_conv(1, sub)
            ks[:, sub] = k_rows
            v_rows = short_conv(2, sub)
            vs[:, sub] = v_rows
            product = k_rows * v_rows
            gated[:, sub] = product
            ghalo_s[:, sub] = product[rows - taps:].astype(BF16)
    over(WIDE, key_value)

    ghalo = to_seq(ghalo_s, ghalo_r, gh_ss, gh_rs, nxt)

    @pl.when(has_next)
    def _():
        ghalo.start()

    for copy in tables[3:]:
        copy.wait()

    per_wide = WIDE // LANES

    def mixed_rows(c, ls):
        spectrum = gspec[:, ls] + dft_half(fw_taps, ghalo_r[:, ls])
        gspec[:, ls] = spectrum
        mixed = dft_wide(inv_tail, times(spectrum, hspec[:, ls]))
        mix[:, ls] = mixed
        gout[:, ls] = (qs[:, ls] * mixed).astype(BF16)

    e_halo = [
        to_seq(ge.at[i, pl.ds(0, EDGE)], ge.at[i, pl.ds(rows, EDGE)], eh_ss.at[i], eh_rs.at[i], prv) for i in range(3)
    ]

    scatter = {}

    def project(r, beside=None):
        def body(c, carry):
            ds = lanes(c, WIDE)
            if beside is not None:
                beside(c, ds)
            term = mm(gout[...], wv[r, :, ds])
            if r & 1:
                psend[r, :, ds] = term.astype(BF16)
            else:
                part[r, :, ds] = term
            return carry
        lax.fori_loop(0, block // WIDE, body, 0)

    def send_sum(r):
        k = low_bit(r)
        scatter[r] = to_tile(psend.at[r], precv.at[r], p_ss.at[r], p_rs.at[r], k)
        scatter[r].start()

    def owner_copy(send, recv, ss, rs, d):
        return to_seq(send.at[(me + d) % n_seq], recv.at[d], ss.at[d], rs.at[d], (me + d) % n_seq)

    def if_owner(index, body):
        if n_own == n_seq:
            body()
        else:
            pl.when(index < n_own)(body)

    def peers(body):
        def step(d, carry):
            body(d)
            return carry
        lax.fori_loop(1, n_seq, step, 0)

    def to_owners(send, recv, ss, rs):
        peers(lambda d: if_owner((me + d) % n_seq, lambda: owner_copy(send, recv, ss, rs, d).start()))

    def from_owner_copy(full, ss, rs, d):
        return to_seq(full.at[me], full.at[me], ss.at[d], rs.at[d], (me + d) % n_seq)

    def owner_sum(send, recv, ss, rs, full, f_ss, f_rs):
        def body():
            def add(d, total):
                owner_copy(send, recv, ss, rs, d).wait_recv()
                return total + recv[d].astype(F32)
            total = lax.fori_loop(1, n_seq, add, send[me].astype(F32))
            full[me] = total.astype(full.dtype)
            peers(lambda d: from_owner_copy(full, f_ss, f_rs, d).start())
        if_owner(me, body)

    def from_owners(full, ss, rs):
        def wait(d):
            source = (me + n_seq - d) % n_seq
            if_owner(source, lambda: to_seq(full.at[source], full.at[source], ss.at[d], rs.at[d], source).wait_recv())
        peers(wait)

    def end_sends(send, recv, ss, rs, full, f_ss, f_rs):
        peers(lambda d: if_owner((me + d) % n_seq, lambda: owner_copy(send, recv, ss, rs, d).wait_send()))
        if_owner(me, lambda: peers(lambda d: from_owner_copy(full, f_ss, f_rs, d).wait_send()))

    medium_set = (msend, mrecv, m_ss, m_rs, mall, ma_ss, ma_rs)
    short_set = (ssend, srecv, s_ss, s_rs, sall, sa_ss, sa_rs)
    def add_sums(r, first, last):
        total = part[r]
        for k in range(first, last):
            scatter[r + (1 << k)].wait_recv()
            total = total + precv[r + (1 << k)].astype(F32)
        return total

    def step_sums(k):
        for r in range(1 << k, n_tile, 2 << k):
            psend[r] = add_sums(r, 0, k).astype(BF16)
            send_sum(r)

    def short_grad(i, c):
        for p, sub in enumerate(parts(c)):
            g_rows = ge[i, pl.ds(0, rows), sub] * scale
            for j in range(short):
                ssend[c * per_wide + p, pl.ds(i * EDGE + j, 1), :] = jnp.sum(
                    g_rows * xe[i, pl.ds(EDGE - j, rows), sub], axis=0, keepdims=True
                )
            for j in range(short, EDGE):
                ssend[c * per_wide + p, pl.ds(i * EDGE + j, 1), :] = jnp.zeros((1, LANES), F32)

    outs = (gq_ref, gk_ref, gv_ref)

    def feature_grad(i, c):
        for sub in parts(c):
            total = sf[i, pl.ds(0, 1), sub] * ge[i, pl.ds(0, rows), sub]
            for j in range(1, short):
                total = total + sf[i, pl.ds(j, 1), sub] * ge[i, pl.ds(j, rows), sub]
            outs[i][:, sub] = total

    for r in range(n_tile):
        if r == 0:
            own_cot.wait()
        else:
            gather[r].wait_recv()
            for k in reversed(range(low_bit(r))):
                slot = r + (1 << k)
                gather[slot] = to_tile(cotv.at[r], cotv.at[slot], ca_ss.at[slot], ca_rs.at[slot], k)
                gather[slot].start()
        if r < 2:
            w_copies[r].wait()
        if r == 2:
            for even in range(2, n_tile, 2):
                project(even)

        def grad_block(c, ls, r=r):
            term = lax.dot_general(
                cotv[r], wv[r, ls, :], (((1,), (1,)), ((), ())), preferred_element_type=F32
            )
            if r > 0:
                term = term + gg[:, ls]
            else:
                gspec[:, ls] = dft_wide(fw_tail, gated[:, ls])
                for sub in parts(c):
                    qs[:, sub] = short_conv(0, sub)
            if r < n_tile - 1:
                gg[:, ls] = term
            else:
                ge[0, pl.ds(0, rows), ls] = term * mix[:, ls]
                grad_mixed = term * qs[:, ls]
                gmix[:, ls] = grad_mixed
                mhalo_s[:, ls] = grad_mixed[:taps].astype(BF16)
        over(WIDE, grad_block)

        if r == 1:
            @pl.when(has_prev)
            def _():
                ghalo.wait_recv()
            over(WIDE, mixed_rows)
            for late in range(2, n_tile):
                w_copies[late].wait()
            for odd in range(n_tile - 1, 0, -2):
                project(odd)
                send_sum(odd)
        if r == 2:
            for k in range(1, bits):
                step_sums(k)

    mhalo = to_seq(mhalo_s, mhalo_r, mh_ss, mh_rs, prv)

    @pl.when(has_prev)
    def _():
        mhalo.start()
        e_halo[0].start()

    def medium_grad(c, ls):
        v_spec = dft_wide(fw_head, gmix[:, ls])
        vspec[:, ls] = v_spec
        terms = (dft_wide(inv_taps, conj_times(gspec[:, ls], v_spec)) * scale).astype(BF16)
        for p in range(per_wide):
            msend[c * per_wide + p] = terms[:, p * LANES:(p + 1) * LANES]
    over(WIDE, medium_grad)
    to_owners(*medium_set[:4])
    project(0, lambda c, ls: short_grad(0, c))

    @pl.when(has_next)
    def _():
        mhalo.wait_recv()
        e_halo[0].wait_recv()

    def product_rows(c, ls):
        spectrum = vspec[:, ls] + dft_half(fw_after, mhalo_r[:, ls])
        grad_prod = dft_wide(inv_head, conj_times(hspec[:, ls], spectrum))
        ge[1, pl.ds(0, rows), ls] = grad_prod * vs[:, ls]
        ge[2, pl.ds(0, rows), ls] = grad_prod * ks[:, ls]
        feature_grad(0, c)

    over(WIDE, product_rows)

    @pl.when(has_prev)
    def _():
        e_halo[1].start()
        e_halo[2].start()

    owner_sum(*medium_set)

    def last_short(c, ls):
        short_grad(1, c)
        short_grad(2, c)

    over(WIDE, last_short)
    to_owners(*short_set[:4])

    @pl.when(has_next)
    def _():
        e_halo[1].wait_recv()
        e_halo[2].wait_recv()

    def last_features(c, ls):
        feature_grad(1, c)
        feature_grad(2, c)
    over(WIDE, last_features)

    owner_sum(*short_set)
    out_ref[...] = add_sums(0, 0, bits)

    from_owners(mall, ma_ss, ma_rs)
    from_owners(sall, sa_ss, sa_rs)

    for o in range(n_own):
        columns = slice(o * LANES, (o + 1) * LANES)
        gm_ref[:, columns] = mall[o].astype(F32)
        for i in range(3):
            gs_ref[i, :, columns] = sall[o, i * EDGE:i * EDGE + short]

    end_sends(*medium_set)
    end_sends(*short_set)
    for r in range(1, n_tile):
        gather[r].wait_send()
        scatter[r].wait_send()

    @pl.when(has_next)
    def _():
        for i in range(3):
            x_halo[i].wait_send()
        ghalo.wait_send()

    @pl.when(has_prev)
    def _():
        for i in range(3):
            e_halo[i].wait_send()
        mhalo.wait_send()


def write_results(*refs):
    count = len(refs) // 2
    sems = refs[-1]
    copies = [pltpu.make_async_copy(refs[i], refs[count + i], sems.at[i]) for i in range(count)]
    for copy in copies:
        copy.start()
    for copy in copies:
        copy.wait()


def shards(n_seq, n_tile, query_feat, key_feat, value_feat, short_filter, medium_filter, out_weight, cotangent):
    rows, width = query_feat.shape
    short = short_filter.shape[1]
    taps = medium_filter.shape[0]
    block = cotangent.shape[1]
    size = rows + taps
    n_own = width // LANES
    assert width == block and n_tile >= 4
    assert n_own <= n_seq and short <= EDGE and rows >= taps
    scale = 1.0 / math.sqrt(n_seq * rows)
    consts = dft_consts(rows, taps)
    hbm = pl.BlockSpec(memory_space=pltpu.HBM)
    vmem = pl.BlockSpec(memory_space=pltpu.VMEM)
    dma = pltpu.SemaphoreType.DMA
    results = pl.pallas_call(
        functools.partial(kernel, n_seq, n_tile, n_own, scale),
        out_shape=(
            pltpu.VMEM((rows, block), F32),
            pltpu.VMEM((rows, width), F32),
            pltpu.VMEM((rows, width), F32),
            pltpu.VMEM((rows, width), F32),
            pltpu.VMEM(short_filter.shape, F32),
            pltpu.VMEM(medium_filter.shape, F32),
        ),
        in_specs=[hbm] * 14,
        out_specs=[vmem] * 6,
        scratch_shapes=[
            pltpu.VMEM(short_filter.shape, F32),
            pltpu.VMEM(medium_filter.shape, F32),
            *[pltpu.VMEM(c.shape, BF16) for c in consts],
            pltpu.VMEM((3, rows + EDGE, width), F32),
            pltpu.VMEM((n_tile, width, block), BF16),
            pltpu.VMEM((n_tile, rows, block), BF16),
            pltpu.VMEM((size, width), F32),
            pltpu.VMEM((size, width), F32),
            pltpu.VMEM((size, width), F32),
            pltpu.VMEM((rows, width), F32),
            pltpu.VMEM((rows, width), F32),
            pltpu.VMEM((rows, width), F32),
            pltpu.VMEM((rows, width), F32),
            pltpu.VMEM((rows, width), F32),
            pltpu.VMEM((rows, width), F32),
            pltpu.VMEM((rows, width), F32),
            pltpu.VMEM((3, rows + EDGE, width), F32),
            pltpu.VMEM((rows, width), BF16),
            pltpu.VMEM((n_tile, rows, block), F32),
            pltpu.VMEM((taps, width), BF16),
            pltpu.VMEM((taps, width), BF16),
            pltpu.VMEM((taps, width), BF16),
            pltpu.VMEM((taps, width), BF16),
            pltpu.VMEM((n_tile, rows, block), BF16),
            pltpu.VMEM((n_tile, rows, block), BF16),
            pltpu.VMEM((n_own, taps, LANES), BF16),
            pltpu.VMEM((n_seq, taps, LANES), BF16),
            pltpu.VMEM((n_own, taps, LANES), BF16),
            pltpu.VMEM((n_own, 3 * EDGE, LANES), F32),
            pltpu.VMEM((n_seq, 3 * EDGE, LANES), F32),
            pltpu.VMEM((n_own, 3 * EDGE, LANES), F32),
            dma((9,)),
            dma((3,)),
            dma((n_tile,)),
            dma,
            dma((3,)),
            dma((3,)),
            dma((n_tile,)),
            dma((n_tile,)),
            dma,
            dma,
            dma,
            dma,
            dma((3,)),
            dma((3,)),
            dma((n_tile,)),
            dma((n_tile,)),
            *[dma((n_seq,)) for _ in range(8)],
        ],
        compiler_params=pltpu.CompilerParams(
            collective_id=0, has_side_effects=True, vmem_limit_bytes=60 * 1024 * 1024
        ),
    )(
        query_feat, key_feat, value_feat, cotangent, out_weight, short_filter, medium_filter,
        *[jnp.asarray(c) for c in consts],
    )
    return pl.pallas_call(
        write_results,
        out_shape=tuple(jax.ShapeDtypeStruct(r.shape, r.dtype) for r in results),
        in_specs=[pl.BlockSpec(memory_space=pl.ANY)] * len(results),
        out_specs=[hbm] * len(results),
        scratch_shapes=[dma((len(results),))],
        compiler_params=pltpu.CompilerParams(vmem_limit_bytes=8 * 1024 * 1024),
    )(*results)


def solution(mesh):
    in_specs = (
        P("seq", "tile"),
        P("seq", "tile"),
        P("seq", "tile"),
        P(None, None, "tile"),
        P(None, "tile"),
        P("tile", None),
        P("seq", "tile"),
    )
    out_specs = (
        P("seq", "tile"),
        P("seq", "tile"),
        P("seq", "tile"),
        P("seq", "tile"),
        P(None, None, "tile"),
        P(None, "tile"),
    )
    body = functools.partial(shards, mesh.shape["seq"], mesh.shape["tile"])
    return jax.shard_map(body, mesh=mesh, in_specs=in_specs, out_specs=out_specs, check_vma=False)
```

```python
import functools
import math

import jax
import jax.numpy as jnp
import ml_dtypes
import numpy as np
from jax import lax
from jax.experimental import pallas as pl
from jax.experimental.pallas import tpu as pltpu
from jax.sharding import PartitionSpec as P

MESH = pl.DeviceIdType.MESH
F32 = jnp.float32
BF16 = jnp.bfloat16
LANES = 128
WIDE = 256
EDGE = 8


def split_const(matrix, wide=True):
    hi = matrix.astype(np.float32).astype(ml_dtypes.bfloat16)
    lo = (matrix - hi.astype(np.float64)).astype(np.float32).astype(ml_dtypes.bfloat16)
    return np.concatenate([hi, lo, hi] if wide else [hi, lo], axis=1)


def dft_consts(rows, taps):
    size = rows + taps
    theta = 2.0 * np.pi * (np.arange(size // 2) + 0.5) / size

    def forward(first, last, wide=True):
        angle = theta[:, None] * np.arange(first, last)[None, :]
        return split_const(np.concatenate([np.cos(angle), -np.sin(angle)], axis=0), wide)

    def inverse(first, last):
        angle = np.arange(first, last)[:, None] * theta[None, :]
        return split_const(np.concatenate([np.cos(angle), -np.sin(angle)], axis=1) * (2.0 / size))

    return (
        forward(0, taps),
        forward(taps, size),
        forward(0, rows),
        forward(rows, size, False),
        inverse(taps, size),
        inverse(0, rows),
        inverse(-taps, 0),
    )


def mm(a, b):
    return jnp.dot(a, b, preferred_element_type=F32)


def dft_wide(matrix, x):
    hi = x.astype(BF16)
    lo = (x - hi.astype(F32)).astype(BF16)
    return mm(matrix[...], jnp.concatenate([hi, hi, lo], axis=0))


def dft_half(matrix, x):
    return mm(matrix[:, :2 * x.shape[0]], jnp.concatenate([x, x], axis=0))


def times(a, b):
    half = a.shape[0] // 2
    ar, ai, br, bi = a[:half], a[half:], b[:half], b[half:]
    return jnp.concatenate([ar * br - ai * bi, ar * bi + ai * br], axis=0)


def conj_times(a, b):
    half = a.shape[0] // 2
    ar, ai, br, bi = a[:half], a[half:], b[:half], b[half:]
    return jnp.concatenate([ar * br + ai * bi, ar * bi - ai * br], axis=0)


def low_bit(r):
    return (r & -r).bit_length() - 1


def kernel(
    n_seq, n_tile, n_own, scale,
    xq, xk, xv, cot, weight, sf_in, mf_in, fw_taps_in, fw_tail_in, fw_head_in, fw_after_in, inv_tail_in,
    inv_head_in, inv_taps_in,
    out_ref, gq_ref, gk_ref, gv_ref, gs_ref, gm_ref,
    sf, mf, fw_taps, fw_tail, fw_head, fw_after, inv_tail, inv_head, inv_taps,
    xe, wv, cotv, hspec, gspec, vspec, ks, vs, qs, gated, gg, gmix, ge, gout, part,
    ghalo_s, ghalo_r, mhalo_s, mhalo_r, psend, precv, msend, mrecv, mall, ssend, srecv, sall,
    t_sem, x_sem, w_sem, c_sem, xh_ss, xh_rs, ca_ss, ca_rs, gh_ss, gh_rs, mh_ss, mh_rs,
    eh_ss, eh_rs, p_ss, p_rs, m_ss, m_rs, ma_ss, ma_rs, s_ss, s_rs, sa_ss, sa_rs,
):
    rows, width = ks.shape
    taps = mf.shape[0]
    short = sf.shape[1]
    block = cotv.shape[2]
    bits = n_tile.bit_length() - 1
    x_refs = (xq, xk, xv)
    me = lax.axis_index("seq")
    tile = lax.axis_index("tile")

    def flip(k):
        return tile + (1 << k) - (2 << k) * ((tile // (1 << k)) % 2)

    def relative(r):
        index = tile * 0
        for k in range(bits):
            bit = (tile // (1 << k)) % 2
            index = index + (1 << k) * ((1 - bit) if (r >> k) & 1 else bit)
        return index

    def to_seq(src, dst, send, recv, index):
        return pltpu.make_async_remote_copy(src, dst, send, recv, device_id={"seq": index}, device_id_type=MESH)

    def to_tile(src, dst, send, recv, k):
        return pltpu.make_async_remote_copy(src, dst, send, recv, device_id={"tile": flip(k)}, device_id_type=MESH)

    def lanes(c, size):
        return pl.ds(pl.multiple_of(c * size, size), size)

    def over(size, body):
        def step(c, carry):
            body(c, lanes(c, size))
            return carry
        lax.fori_loop(0, width // size, step, 0)

    table_pairs = (
        (mf_in, mf), (fw_taps_in, fw_taps), (sf_in, sf), (fw_tail_in, fw_tail), (fw_head_in, fw_head),
        (fw_after_in, fw_after), (inv_tail_in, inv_tail), (inv_head_in, inv_head), (inv_taps_in, inv_taps),
    )
    tables = [pltpu.make_async_copy(pair[0], pair[1], t_sem.at[i]) for i, pair in enumerate(table_pairs)]
    for copy in tables[:3]:
        copy.start()
    x_copies = [pltpu.make_async_copy(x_refs[i], xe.at[i, pl.ds(EDGE, rows)], x_sem.at[i]) for i in range(3)]
    for copy in x_copies:
        copy.start()
    own_cot = pltpu.make_async_copy(cot, cotv.at[0], c_sem)
    own_cot.start()
    barrier = pltpu.get_barrier_semaphore()

    def greet(d, carry):
        pl.semaphore_signal(barrier, inc=1, device_id={"seq": (me + d) % n_seq}, device_id_type=MESH)
        return carry
    lax.fori_loop(1, n_seq, greet, 0)
    for k in range(bits):
        pl.semaphore_signal(barrier, inc=1, device_id={"tile": flip(k)}, device_id_type=MESH)
    pl.semaphore_wait(barrier, n_seq - 1 + bits)

    has_next = me < n_seq - 1
    has_prev = me > 0
    nxt = (me + 1) % n_seq
    prv = (me + n_seq - 1) % n_seq

    x_halo = [
        to_seq(x_refs[i].at[pl.ds(rows - EDGE, EDGE)], xe.at[i, pl.ds(0, EDGE)], xh_ss.at[i], xh_rs.at[i], nxt)
        for i in range(3)
    ]

    @pl.when(has_next)
    def _():
        for i in (1, 2, 0):
            x_halo[i].start()

    gather = {}
    for k in reversed(range(bits)):
        gather[1 << k] = to_tile(cot, cotv.at[1 << k], ca_ss.at[1 << k], ca_rs.at[1 << k], k)
        gather[1 << k].start()

    for copy in tables[3:]:
        copy.start()
    w_copies = []
    for r in range(n_tile):
        columns = pl.ds(pl.multiple_of(relative(r) * block, block), block)
        w_copies.append(pltpu.make_async_copy(weight.at[:, columns], wv.at[r], w_sem.at[r]))
        w_copies[-1].start()

    @pl.when(jnp.logical_not(has_prev))
    def _():
        for i in range(3):
            xe[i, pl.ds(0, EDGE), :] = jnp.zeros((EDGE, width), F32)
        ghalo_r[...] = jnp.zeros_like(ghalo_r)

    @pl.when(jnp.logical_not(has_next))
    def _():
        for i in range(3):
            ge[i, pl.ds(rows, EDGE), :] = jnp.zeros((EDGE, width), F32)
        mhalo_r[...] = jnp.zeros_like(mhalo_r)

    for copy in tables[:3]:
        copy.wait()

    def filter_spectrum(c, ls):
        hspec[:, ls] = dft_wide(fw_taps, mf[:, ls])
    over(WIDE, filter_spectrum)

    for copy in x_copies:
        copy.wait()

    @pl.when(has_prev)
    def _():
        for i in range(3):
            x_halo[i].wait_recv()

    def short_conv(i, ls):
        total = sf[i, pl.ds(0, 1), ls] * xe[i, pl.ds(EDGE, rows), ls]
        for j in range(1, short):
            total = total + sf[i, pl.ds(j, 1), ls] * xe[i, pl.ds(EDGE - j, rows), ls]
        return total

    def key_value(c, ls):
        k_rows = short_conv(1, ls)
        ks[:, ls] = k_rows
        v_rows = short_conv(2, ls)
        vs[:, ls] = v_rows
        product = k_rows * v_rows
        gated[:, ls] = product
        ghalo_s[:, ls] = product[rows - taps:].astype(BF16)
    over(LANES, key_value)

    ghalo = to_seq(ghalo_s, ghalo_r, gh_ss, gh_rs, nxt)

    @pl.when(has_next)
    def _():
        ghalo.start()

    def query(c, ls):
        qs[:, ls] = short_conv(0, ls)
    over(LANES, query)

    for copy in tables[3:]:
        copy.wait()

    def gated_spectrum(c, ls):
        gspec[:, ls] = dft_wide(fw_tail, gated[:, ls])
    over(WIDE, gated_spectrum)

    for r in range(n_tile):
        if r == 0:
            own_cot.wait()
        else:
            gather[r].wait_recv()
            for k in reversed(range(low_bit(r))):
                slot = r + (1 << k)
                gather[slot] = to_tile(cotv.at[r], cotv.at[slot], ca_ss.at[slot], ca_rs.at[slot], k)
                gather[slot].start()
        w_copies[r].wait()

        def grad_block(c, ls, r=r):
            term = lax.dot_general(
                cotv[r], wv[r, ls, :], (((1,), (1,)), ((), ())), preferred_element_type=F32
            )
            if r > 0:
                term = term + gg[:, ls]
            gg[:, ls] = term
            if r == n_tile - 1:
                grad_mixed = term * qs[:, ls]
                gmix[:, ls] = grad_mixed
                mhalo_s[:, ls] = grad_mixed[:taps].astype(BF16)
        over(WIDE, grad_block)

    mhalo = to_seq(mhalo_s, mhalo_r, mh_ss, mh_rs, prv)

    @pl.when(has_prev)
    def _():
        mhalo.start()

    @pl.when(has_prev)
    def _():
        ghalo.wait_recv()

    def mixed_rows(c, ls):
        spectrum = gspec[:, ls] + dft_half(fw_taps, ghalo_r[:, ls])
        gspec[:, ls] = spectrum
        mixed = dft_wide(inv_tail, times(spectrum, hspec[:, ls]))
        gout[:, ls] = (qs[:, ls] * mixed).astype(BF16)
        ge[0, pl.ds(0, rows), ls] = gg[:, ls] * mixed
    over(WIDE, mixed_rows)

    e_halo = [
        to_seq(ge.at[i, pl.ds(0, EDGE)], ge.at[i, pl.ds(rows, EDGE)], eh_ss.at[i], eh_rs.at[i], prv) for i in range(3)
    ]

    @pl.when(has_prev)
    def _():
        e_halo[0].start()

    scatter = {}

    def project(r):
        def body(c, carry):
            ds = lanes(c, WIDE)
            term = mm(gout[...], wv[r, :, ds])
            if r & 1:
                psend[r, :, ds] = term.astype(BF16)
            else:
                part[r, :, ds] = term
            return carry
        lax.fori_loop(0, block // WIDE, body, 0)

    def send_sum(r):
        k = low_bit(r)
        scatter[r] = to_tile(psend.at[r], precv.at[r], p_ss.at[r], p_rs.at[r], k)
        scatter[r].start()

    per_wide = WIDE // LANES

    def medium_grad(c, ls):
        v_spec = dft_wide(fw_head, gmix[:, ls])
        vspec[:, ls] = v_spec
        terms = dft_wide(inv_taps, conj_times(gspec[:, ls], v_spec)) * scale
        for p in range(per_wide):
            msend[c * per_wide + p] = terms[:, p * LANES:(p + 1) * LANES].astype(BF16)
    over(WIDE, medium_grad)

    def owner_copy(send, recv, ss, rs, d):
        return to_seq(send.at[(me + d) % n_seq], recv.at[d], ss.at[d], rs.at[d], (me + d) % n_seq)

    def if_owner(index, body):
        if n_own == n_seq:
            body()
        else:
            pl.when(index < n_own)(body)

    def peers(body):
        def step(d, carry):
            body(d)
            return carry
        lax.fori_loop(1, n_seq, step, 0)

    def to_owners(send, recv, ss, rs):
        peers(lambda d: if_owner((me + d) % n_seq, lambda: owner_copy(send, recv, ss, rs, d).start()))

    def from_owner_copy(full, ss, rs, d):
        return to_seq(full.at[me], full.at[me], ss.at[d], rs.at[d], (me + d) % n_seq)

    def owner_sum(send, recv, ss, rs, full, f_ss, f_rs):
        def body():
            def add(d, total):
                owner_copy(send, recv, ss, rs, d).wait_recv()
                return total + recv[d].astype(F32)
            total = lax.fori_loop(1, n_seq, add, send[me].astype(F32))
            full[me] = total.astype(full.dtype)
            peers(lambda d: from_owner_copy(full, f_ss, f_rs, d).start())
        if_owner(me, body)

    def from_owners(full, ss, rs):
        def wait(d):
            source = (me + n_seq - d) % n_seq
            if_owner(source, lambda: to_seq(full.at[source], full.at[source], ss.at[d], rs.at[d], source).wait_recv())
        peers(wait)

    def end_sends(send, recv, ss, rs, full, f_ss, f_rs):
        peers(lambda d: if_owner((me + d) % n_seq, lambda: owner_copy(send, recv, ss, rs, d).wait_send()))
        if_owner(me, lambda: peers(lambda d: from_owner_copy(full, f_ss, f_rs, d).wait_send()))

    medium_set = (msend, mrecv, m_ss, m_rs, mall, ma_ss, ma_rs)
    short_set = (ssend, srecv, s_ss, s_rs, sall, sa_ss, sa_rs)
    to_owners(*medium_set[:4])

    def add_sums(r, first, last):
        total = part[r]
        for k in range(first, last):
            scatter[r + (1 << k)].wait_recv()
            total = total + precv[r + (1 << k)].astype(F32)
        return total

    def step_sums(k):
        for r in range(1 << k, n_tile, 2 << k):
            psend[r] = add_sums(r, 0, k).astype(BF16)
            send_sum(r)

    for r in range(n_tile - 1, 0, -2):
        project(r)
        send_sum(r)

    @pl.when(has_next)
    def _():
        mhalo.wait_recv()

    def product_rows(c, ls):
        spectrum = vspec[:, ls] + dft_half(fw_after, mhalo_r[:, ls])
        grad_prod = dft_wide(inv_head, conj_times(hspec[:, ls], spectrum))
        ge[1, pl.ds(0, rows), ls] = grad_prod * vs[:, ls]
        ge[2, pl.ds(0, rows), ls] = grad_prod * ks[:, ls]
    over(WIDE, product_rows)

    @pl.when(has_prev)
    def _():
        e_halo[1].start()
        e_halo[2].start()

    for r in range(2, n_tile, 2):
        project(r)
    for k in range(1, bits):
        step_sums(k)
    project(0)
    owner_sum(*medium_set)

    def short_grad(c, ls):
        for i in range(3):
            g_rows = ge[i, pl.ds(0, rows), ls] * scale
            for j in range(short):
                ssend[c, pl.ds(i * EDGE + j, 1), :] = jnp.sum(
                    g_rows * xe[i, pl.ds(EDGE - j, rows), ls], axis=0, keepdims=True
                )
            for j in range(short, EDGE):
                ssend[c, pl.ds(i * EDGE + j, 1), :] = jnp.zeros((1, LANES), F32)
    over(LANES, short_grad)
    to_owners(*short_set[:4])

    @pl.when(has_next)
    def _():
        for i in range(3):
            e_halo[i].wait_recv()

    outs = (gq_ref, gk_ref, gv_ref)

    def feature_grad(c, ls):
        for i in range(3):
            total = sf[i, pl.ds(0, 1), ls] * ge[i, pl.ds(0, rows), ls]
            for j in range(1, short):
                total = total + sf[i, pl.ds(j, 1), ls] * ge[i, pl.ds(j, rows), ls]
            outs[i][:, ls] = total
    over(LANES, feature_grad)

    owner_sum(*short_set)
    out_ref[...] = add_sums(0, 0, bits)

    from_owners(mall, ma_ss, ma_rs)
    from_owners(sall, sa_ss, sa_rs)

    for o in range(n_own):
        columns = slice(o * LANES, (o + 1) * LANES)
        gm_ref[:, columns] = mall[o].astype(F32)
        for i in range(3):
            gs_ref[i, :, columns] = sall[o, i * EDGE:i * EDGE + short]

    end_sends(*medium_set)
    end_sends(*short_set)
    for r in range(1, n_tile):
        gather[r].wait_send()
        scatter[r].wait_send()

    @pl.when(has_next)
    def _():
        for i in range(3):
            x_halo[i].wait_send()
        ghalo.wait_send()

    @pl.when(has_prev)
    def _():
        for i in range(3):
            e_halo[i].wait_send()
        mhalo.wait_send()


def write_results(*refs):
    count = len(refs) // 2
    sems = refs[-1]
    copies = [pltpu.make_async_copy(refs[i], refs[count + i], sems.at[i]) for i in range(count)]
    for copy in copies:
        copy.start()
    for copy in copies:
        copy.wait()


def shards(n_seq, n_tile, query_feat, key_feat, value_feat, short_filter, medium_filter, out_weight, cotangent):
    rows, width = query_feat.shape
    short = short_filter.shape[1]
    taps = medium_filter.shape[0]
    block = cotangent.shape[1]
    size = rows + taps
    n_own = width // LANES
    assert n_own <= n_seq and short <= EDGE and rows >= taps
    scale = 1.0 / math.sqrt(n_seq * rows)
    consts = dft_consts(rows, taps)
    hbm = pl.BlockSpec(memory_space=pltpu.HBM)
    vmem = pl.BlockSpec(memory_space=pltpu.VMEM)
    dma = pltpu.SemaphoreType.DMA
    results = pl.pallas_call(
        functools.partial(kernel, n_seq, n_tile, n_own, scale),
        out_shape=(
            pltpu.VMEM((rows, block), F32),
            pltpu.VMEM((rows, width), F32),
            pltpu.VMEM((rows, width), F32),
            pltpu.VMEM((rows, width), F32),
            pltpu.VMEM(short_filter.shape, F32),
            pltpu.VMEM(medium_filter.shape, F32),
        ),
        in_specs=[hbm] * 14,
        out_specs=[vmem] * 6,
        scratch_shapes=[
            pltpu.VMEM(short_filter.shape, F32),
            pltpu.VMEM(medium_filter.shape, F32),
            *[pltpu.VMEM(c.shape, BF16) for c in consts],
            pltpu.VMEM((3, rows + EDGE, width), F32),
            pltpu.VMEM((n_tile, width, block), BF16),
            pltpu.VMEM((n_tile, rows, block), BF16),
            pltpu.VMEM((size, width), F32),
            pltpu.VMEM((size, width), F32),
            pltpu.VMEM((size, width), F32),
            pltpu.VMEM((rows, width), F32),
            pltpu.VMEM((rows, width), F32),
            pltpu.VMEM((rows, width), F32),
            pltpu.VMEM((rows, width), F32),
            pltpu.VMEM((rows, width), F32),
            pltpu.VMEM((rows, width), F32),
            pltpu.VMEM((3, rows + EDGE, width), F32),
            pltpu.VMEM((rows, width), BF16),
            pltpu.VMEM((n_tile, rows, block), F32),
            pltpu.VMEM((taps, width), BF16),
            pltpu.VMEM((taps, width), BF16),
            pltpu.VMEM((taps, width), BF16),
            pltpu.VMEM((taps, width), BF16),
            pltpu.VMEM((n_tile, rows, block), BF16),
            pltpu.VMEM((n_tile, rows, block), BF16),
            pltpu.VMEM((n_own, taps, LANES), BF16),
            pltpu.VMEM((n_seq, taps, LANES), BF16),
            pltpu.VMEM((n_own, taps, LANES), BF16),
            pltpu.VMEM((n_own, 3 * EDGE, LANES), F32),
            pltpu.VMEM((n_seq, 3 * EDGE, LANES), F32),
            pltpu.VMEM((n_own, 3 * EDGE, LANES), F32),
            dma((9,)),
            dma((3,)),
            dma((n_tile,)),
            dma,
            dma((3,)),
            dma((3,)),
            dma((n_tile,)),
            dma((n_tile,)),
            dma,
            dma,
            dma,
            dma,
            dma((3,)),
            dma((3,)),
            dma((n_tile,)),
            dma((n_tile,)),
            *[dma((n_seq,)) for _ in range(8)],
        ],
        compiler_params=pltpu.CompilerParams(
            collective_id=0, has_side_effects=True, vmem_limit_bytes=60 * 1024 * 1024
        ),
    )(
        query_feat, key_feat, value_feat, cotangent, out_weight, short_filter, medium_filter,
        *[jnp.asarray(c) for c in consts],
    )
    return pl.pallas_call(
        write_results,
        out_shape=tuple(jax.ShapeDtypeStruct(r.shape, r.dtype) for r in results),
        in_specs=[pl.BlockSpec(memory_space=pl.ANY)] * len(results),
        out_specs=[hbm] * len(results),
        scratch_shapes=[dma((len(results),))],
        compiler_params=pltpu.CompilerParams(vmem_limit_bytes=8 * 1024 * 1024),
    )(*results)


def solution(mesh):
    in_specs = (
        P("seq", "tile"),
        P("seq", "tile"),
        P("seq", "tile"),
        P(None, None, "tile"),
        P(None, "tile"),
        P("tile", None),
        P("seq", "tile"),
    )
    out_specs = (
        P("seq", "tile"),
        P("seq", "tile"),
        P("seq", "tile"),
        P("seq", "tile"),
        P(None, None, "tile"),
        P(None, "tile"),
    )
    body = functools.partial(shards, mesh.shape["seq"], mesh.shape["tile"])
    return jax.shard_map(body, mesh=mesh, in_specs=in_specs, out_specs=out_specs, check_vma=False)
```
